32 devices in a mesh: group: 16 (over z, y, core), tok: 2 (over x).
Axes of the slice: x: 2, y: 2, z: 4, core: 2. Of those that a mesh axis runs over, the one named last changes fastest.
Arguments:
- latents: bfloat16 [4096, 5120], P(('group', 'tok')), may hold values from -6 to 6
- timesteps: int32 [16], P('group'), may hold values from 0 to 999
- mod_shift: float32 [5120], replicated, may hold values from -3 to 3
- mod_scale: float32 [5120], replicated, may hold values from -1.5 to 1.5
- w_query: bfloat16 [5120, 3072], P('group', 'tok'), may hold values from -7 to 7
- w_key: bfloat16 [5120, 3072], P('group', 'tok'), may hold values from -7 to 7
- w_value: bfloat16 [5120, 3072], P('group', 'tok'), may hold values from -0.078125 to 0.078125
- query_gain: float32 [3072], P('tok'), may hold values from 0.5 to 1.5
- key_gain: float32 [3072], P('tok'), may hold values from 0.5 to 1.5
- cache_keys: bfloat16 [4096, 3072], P('group', 'tok'), may hold values from -85 to 85
- cache_values: bfloat16 [4096, 3072], P('group', 'tok'), may hold values from -6 to 6
- owners: int32 [16], replicated, may hold values from 0 to 15, each once
- tile_mask: int32 [24, 2, 6], P('tok'), may hold values from 0 to 1, as said below
Outputs:
- attended: bfloat16 [4096, 3072], P('group', 'tok')
The draws below stay inside these ranges and needn't reach their ends.
Inputs may be any that keep to these rules, and one draw needn't show every extreme that they name: `tile_mask`: each query tile i of each head sees 1 to 6 key tiles, always tile 2 * 2 + i; some query tile sees exactly 6.
All inputs are finite; a program needn't handle non-finite values.
Results may differ from the reference program's by a relative error of at most 0.012.
The reference program's roundings to bfloat16 on the way count: a program that leaves them out, or rounds other values in their place, can miss the bound.
Values may be sent and summed in bfloat16 or wider, within the bound.
A program may use at most 128 MiB of HBM per device.

```python
import math
import jax
import jax.numpy as jnp
from jax import lax

D = 5120
HEADS = 24
HEAD_DIM = 128
TILE = 128
GROUP_ROWS = 256
N_GROUP_ROWS_ALL = 4096
QTILES = 2
KTILES = 6
MOST = 6
N_GROUP = 16


def rising_weight(key, salt):
    base = jnp.clip(jax.random.normal(jax.random.fold_in(key, salt), (D, HEADS * HEAD_DIM), jnp.float32), -6.0, 6.0)
    head_index = (jnp.arange(HEADS * HEAD_DIM) // HEAD_DIM).astype(jnp.float32)
    rising = jnp.exp(math.log(3.0) * head_index / max(HEADS - 1, 1))
    return (base * rising * D ** (-0.5)).astype(jnp.bfloat16)


def draw_w_query(key, part):
    return rising_weight(key, 11)


def draw_w_key(key, part):
    return rising_weight(key, 23)


def draw_cache_keys(key, part):
    shape = (N_GROUP * GROUP_ROWS, HEADS * HEAD_DIM)
    first_key = jax.random.fold_in(key, 31)
    values = jnp.clip(jax.random.normal(first_key, shape, jnp.float32), -4.0, 4.0)
    return values.astype(jnp.bfloat16)


def draw_tile_mask(key, part):
    base_key = jax.random.fold_in(key, 51)
    jitter_key = jax.random.fold_in(key, 52)
    spot_key = jax.random.fold_in(key, 53)
    order_key = jax.random.fold_in(key, 54)
    base_count = jax.random.randint(base_key, (HEADS, 1), 1, MOST - 1)
    jitter = jax.random.randint(jitter_key, (HEADS, QTILES), 0, 3)
    counts = jnp.minimum(base_count + jitter, MOST)
    spot = jax.random.randint(spot_key, (), 0, HEADS * QTILES)
    flat_index = jnp.arange(HEADS * QTILES).reshape(HEADS, QTILES)
    counts = jnp.where(flat_index == spot, MOST, counts)
    priority = jax.random.randint(order_key, (HEADS, QTILES, KTILES), 0, 1 << 20) * KTILES + jnp.arange(KTILES)[None, None, :]
    diagonal = jnp.arange(KTILES)[None, None, :] == (2 * QTILES + jnp.arange(QTILES))[None, :, None]
    priority = jnp.where(diagonal, 1 << 30, priority)
    ranks = jnp.argsort(jnp.argsort(-priority, axis=-1, stable=True), axis=-1, stable=True)
    return (ranks < counts[:, :, None]).astype(jnp.int32)


def plant(array, key, least, largest):
    longest = array.shape.index(max(array.shape))
    spots = []
    for shift in (0, 1):
        where = [jax.random.randint(jax.random.fold_in(key, axis), (), 0, length) for axis, length in enumerate(array.shape)]
        where[longest] = (where[longest] + shift) % array.shape[longest]
        spots.append(tuple(where))
    return array.at[spots[0]].set(least).at[spots[1]].set(largest)


def levels(stream_key, dims, split, smallest, high):
    def one(axis_at, parts):
        draws = jax.random.uniform(jax.random.fold_in(jax.random.fold_in(stream_key, 6), axis_at), (parts,), jnp.float32, smallest / len(split), high / len(split))
        return jnp.repeat(jnp.exp(draws), dims[axis_at] // parts).reshape((-1,) + (1,) * (len(dims) - axis_at - 1))

    factor_of = one(*split[0])
    for cut in split[1:]:
        factor_of = factor_of * one(*cut)
    return factor_of


def noise(key, dims, scale, most, shards=(), held_as=jnp.bfloat16):
    level = levels(key, dims, shards, -0.22, 0.18) if shards else 1.0
    array = jax.random.normal(key, dims, jnp.float32) * scale * level
    return jnp.minimum(jnp.maximum(array, -most), most).astype(held_as)


def setup_inputs(seed: int = 0) -> dict:
    key_of = jax.random.split(jax.random.key(seed), 14)
    latents = noise(key_of[0], (N_GROUP_ROWS_ALL, D), 1.0, 6.0, ((0, 32),))
    timesteps = plant(jax.random.randint(key_of[1], (N_GROUP,), 0, 1000), jax.random.fold_in(key_of[1], 1), 0, 999).astype(jnp.int32)
    mod_shift = noise(key_of[2], (D,), 0.5, 3.0, (), jnp.float32)
    mod_scale = noise(key_of[3], (D,), 0.3, 1.5, (), jnp.float32)
    w_query = draw_w_query(jax.random.fold_in(key_of[13], 71), 0)
    w_key = draw_w_key(jax.random.fold_in(key_of[13], 71), 0)
    w_value = noise(key_of[6], (D, HEADS * HEAD_DIM), D ** -0.5, 0.078125, ((0, 16), (1, 2)))
    query_gain = jnp.clip(1.0 + 0.1 * jax.random.normal(key_of[7], (HEADS * HEAD_DIM,), jnp.float32), 0.5, 1.5)
    key_gain = jnp.clip(1.0 + 0.1 * jax.random.normal(key_of[8], (HEADS * HEAD_DIM,), jnp.float32), 0.5, 1.5)
    cache_keys = draw_cache_keys(jax.random.fold_in(key_of[13], 71), 0)
    cache_values = noise(key_of[10], (N_GROUP_ROWS_ALL, HEADS * HEAD_DIM), 1.0, 6.0, ((0, 16), (1, 2)))
    owners = jax.random.permutation(key_of[11], N_GROUP).astype(jnp.int32)
    tile_mask = draw_tile_mask(jax.random.fold_in(key_of[13], 71), 0)
    return {"latents": latents, "timesteps": timesteps, "mod_shift": mod_shift, "mod_scale": mod_scale, "w_query": w_query, "w_key": w_key, "w_value": w_value, "query_gain": query_gain, "key_gain": key_gain, "cache_keys": cache_keys, "cache_values": cache_values, "owners": owners, "tile_mask": tile_mask}


EPSILON = 1e-06

def modulate(rows_block, timestep, mod_shift, mod_scale):
    values = rows_block.astype(jnp.float32)
    width = values.shape[-1]
    centred = values - lax.optimization_barrier(jnp.mean(values, axis=-1, keepdims=True))
    spread = lax.optimization_barrier(jnp.mean(centred * centred, axis=-1, keepdims=True))
    normed = centred * lax.rsqrt(spread + EPSILON)
    freqs = jnp.exp(-math.log(10000.0) * jnp.arange(width, dtype=jnp.float32) / width)
    angles = timestep.astype(jnp.float32) * freqs
    return (normed * (1.0 + mod_scale + 0.5 * jnp.cos(angles)) + mod_shift + 0.5 * jnp.sin(angles)).astype(jnp.bfloat16)

def head_normed(raw, gain):
    squares = lax.optimization_barrier(jnp.mean(raw * raw, axis=-1, keepdims=True))
    return (raw * lax.rsqrt(squares + EPSILON) * gain).astype(jnp.bfloat16)

def reference(latents, timesteps, mod_shift, mod_scale, w_query, w_key, w_value, query_gain, key_gain, cache_keys, cache_values, owners, tile_mask):
    width = HEADS * HEAD_DIM
    score_scale = 1.0 / math.sqrt(HEAD_DIM)

    def project(operands):
        rows_block, timestep = operands
        modulated = modulate(rows_block, timestep, mod_shift, mod_scale)
        raw_query = jnp.dot(modulated, w_query, preferred_element_type=jnp.float32)
        raw_key = jnp.dot(modulated, w_key, preferred_element_type=jnp.float32)
        raw_value = jnp.dot(modulated, w_value, preferred_element_type=jnp.float32)
        return (head_normed(raw_query, query_gain), head_normed(raw_key, key_gain), raw_value.astype(jnp.bfloat16))
    groups = latents.reshape(N_GROUP, GROUP_ROWS, D)
    queries, keys_all, values_all = lax.map(project, (groups, timesteps))
    root = owners[N_GROUP - 1].astype(jnp.int32)
    cached_keys = lax.dynamic_slice_in_dim(cache_keys, root * GROUP_ROWS, GROUP_ROWS, 0)
    cached_values = lax.dynamic_slice_in_dim(cache_values, root * GROUP_ROWS, GROUP_ROWS, 0)
    tile_ids = jnp.arange(KTILES, dtype=jnp.int32)
    earlier_region = (tile_ids >= QTILES) & (tile_ids < 2 * QTILES)

    def one_head(operands):
        query_head, key_head, value_head, head_mask = operands
        row_mask = jnp.repeat(jnp.repeat(head_mask, TILE, axis=0), TILE, axis=1)
        scores = jnp.dot(query_head, key_head.T, preferred_element_type=jnp.float32) * score_scale
        scores = jnp.where(row_mask > 0, scores, -jnp.inf)
        peak = lax.optimization_barrier(jnp.max(scores, axis=-1, keepdims=True))
        weights = jnp.exp(scores - peak)
        low_weights = weights.astype(jnp.bfloat16)
        summed = jnp.dot(low_weights, value_head, preferred_element_type=jnp.float32)
        return (summed / lax.optimization_barrier(jnp.sum(weights, axis=-1, keepdims=True))).astype(jnp.bfloat16)

    def attend_group(group_index):
        earlier = jnp.maximum(group_index - 1, 0)
        context_keys = jnp.concatenate([cached_keys, keys_all[earlier], keys_all[group_index]], axis=0)
        context_values = jnp.concatenate([cached_values, values_all[earlier], values_all[group_index]], axis=0)
        allowed = jnp.where(earlier_region[None, None, :] & (group_index == 0), 0, tile_mask)
        query_heads = queries[group_index].reshape(GROUP_ROWS, HEADS, HEAD_DIM).transpose(1, 0, 2)
        key_heads = context_keys.reshape(3 * GROUP_ROWS, HEADS, HEAD_DIM).transpose(1, 0, 2)
        value_heads = context_values.reshape(3 * GROUP_ROWS, HEADS, HEAD_DIM).transpose(1, 0, 2)
        attended = lax.map(one_head, (query_heads, key_heads, value_heads, allowed))
        return attended.transpose(1, 0, 2).reshape(GROUP_ROWS, width)
    outputs = lax.map(attend_group, jnp.arange(N_GROUP, dtype=jnp.int32))
    return outputs.reshape(N_GROUP * GROUP_ROWS, width)
```

```python
import functools
import math

import jax
import jax.numpy as jnp
from jax import lax
from jax.experimental import pallas as pl
from jax.experimental.pallas import tpu as pltpu
from jax.sharding import PartitionSpec as P

EPSILON = 1e-06
MESH = pl.DeviceIdType.MESH


def from_behind(block, axis, distance):
    devices = range(lax.axis_size(axis))
    route = [(i - distance, i) for i in devices if i - distance in devices]
    return lax.ppermute(block, axis, route)


def spread_2(value, axis, source):
    kept = jnp.where(lax.axis_index(axis) == source, value, 0).astype(value.dtype)
    return lax.psum(kept, axis)


def modulate(rows_block, timestep, mod_shift, mod_scale):
    values = rows_block.astype(jnp.float32)
    width = values.shape[-1]
    centred = values - jnp.mean(values, axis=-1, keepdims=True)
    spread = jnp.mean(centred * centred, axis=-1, keepdims=True)
    normed = centred * lax.rsqrt(spread + EPSILON)
    freqs = jnp.exp(-math.log(10000.0) * jnp.arange(width, dtype=jnp.float32) / width)
    angles = timestep.astype(jnp.float32) * freqs
    return (
        normed * (1.0 + mod_scale + 0.5 * jnp.cos(angles)) + mod_shift + 0.5 * jnp.sin(angles)
    ).astype(jnp.bfloat16)


def scaled_rows(raw, squares, width, gain):
    return (raw * lax.rsqrt(squares / width + EPSILON)[:, None] * gain).astype(jnp.bfloat16)


def dense_attention(query_heads, key_heads, value_heads, allowed, tile_rows, score_scale):
    group_rows = query_heads.shape[1]
    block_rows = 512 if group_rows % 512 == 0 else group_rows
    block_count = group_rows // block_rows
    tiles_per_block = block_rows // tile_rows

    def one_head(operands):
        query_head, key_head, value_head, head_mask = operands
        key_mask = jnp.repeat(head_mask, tile_rows, axis=1)

        def one_block(block_index):
            block_queries = lax.dynamic_slice_in_dim(
                query_head, block_index * block_rows, block_rows, 0
            )
            block_mask = lax.dynamic_slice_in_dim(
                key_mask, block_index * tiles_per_block, tiles_per_block, 0
            )
            row_mask = jnp.repeat(block_mask, tile_rows, axis=0)
            scores = (
                jnp.einsum("id,jd->ij", block_queries, key_head, preferred_element_type=jnp.float32)
                * score_scale
            )
            scores = jnp.where(row_mask > 0, scores, -jnp.inf)
            peak = jnp.max(scores, axis=-1, keepdims=True)
            weights = jnp.exp(scores - peak)
            summed = jnp.dot(
                weights.astype(jnp.bfloat16), value_head, preferred_element_type=jnp.float32
            )
            return (summed / jnp.sum(weights, axis=-1, keepdims=True)).astype(jnp.bfloat16)

        blocks_out = lax.map(one_block, jnp.arange(block_count, dtype=jnp.int32))
        return blocks_out.reshape(group_rows, query_head.shape[1])

    return lax.map(one_head, (query_heads, key_heads, value_heads, allowed))


def local(
    latents,
    timesteps,
    mod_shift,
    mod_scale,
    w_query,
    w_key,
    w_value,
    query_gain,
    key_gain,
    cache_keys,
    cache_values,
    owners,
    tile_mask,
):
    modulated = modulate(latents, timesteps[0], mod_shift, mod_scale)
    root = owners[owners.shape[0] - 1]
    head_cols = w_query.shape[1]
    slabs = (
        lax.all_gather(w_query, "group", axis=0, tiled=True),
        lax.all_gather(w_key, "group", axis=0, tiled=True),
        lax.all_gather(w_value, "group", axis=0, tiled=True),
    )
    joined = jnp.concatenate(slabs, axis=1)
    projected = jnp.dot(
        lax.all_gather(modulated, "tok", axis=0, tiled=True),
        joined,
        preferred_element_type=jnp.float32,
    )
    raw_query = projected[:, :head_cols]
    raw_key = projected[:, head_cols : 2 * head_cols]
    raw_value = projected[:, 2 * head_cols :]
    query_squares, key_squares = lax.psum(
        (jnp.sum(raw_query * raw_query, axis=1), jnp.sum(raw_key * raw_key, axis=1)), "tok"
    )
    width = head_cols * lax.axis_size("tok")
    query_rows = scaled_rows(raw_query, query_squares, width, query_gain)
    key_rows = scaled_rows(raw_key, key_squares, width, key_gain)
    value_rows = raw_value.astype(jnp.bfloat16)
    earlier_keys, earlier_values = from_behind((key_rows, value_rows), "group", 1)
    cached = (spread_2(cache_keys, "group", root), spread_2(cache_values, "group", root))
    group_rows = query_rows.shape[0]
    local_heads = tile_mask.shape[0]
    query_tiles = tile_mask.shape[1]
    key_tile_count = tile_mask.shape[2]
    tile_rows = group_rows // query_tiles
    head_size = head_cols // local_heads
    score_scale = 1.0 / math.sqrt(head_size)
    context_keys = jnp.concatenate([cached[0], earlier_keys, key_rows], axis=0)
    context_values = jnp.concatenate([cached[1], earlier_values, value_rows], axis=0)
    is_first = lax.axis_index("group") == 0
    tile_ids = jnp.arange(key_tile_count, dtype=jnp.int32)
    earlier_region = (tile_ids >= query_tiles) & (tile_ids < 2 * query_tiles)
    allowed = jnp.where(earlier_region[None, None, :] & is_first, 0, tile_mask)
    query_heads = query_rows.reshape(group_rows, local_heads, head_size).transpose(1, 0, 2)
    key_heads = context_keys.reshape(3 * group_rows, local_heads, head_size).transpose(1, 0, 2)
    value_heads = context_values.reshape(3 * group_rows, local_heads, head_size).transpose(1, 0, 2)
    attended = dense_attention(query_heads, key_heads, value_heads, allowed, tile_rows, score_scale)
    return attended.transpose(1, 0, 2).reshape(group_rows, head_cols)


AXES = ("zh", "zl", "y", "c", "x")


def gather_kernel(wq_ref, wk_ref, wv_ref, m_ref, gw_ref, ga_ref, ws, wr, ys, yr, as_, ar, ls):
    zh, zl, y, c, x = (lax.axis_index(a) for a in AXES)
    weights = (wq_ref, wk_ref, wv_ref)
    rows = wq_ref.shape[0]
    cols = gw_ref.shape[2] // 3

    def flipped(f):
        return (
            1 - zh if f & 4 else zh,
            1 - zl if f & 2 else zl,
            1 - c if f & 1 else c,
        )

    def place(fzh, fzl, fy, fc):
        return ((fzh * 2 + fzl) * 2 + fy) * 2 + fc

    barrier = pltpu.get_barrier_semaphore()
    partners = [(a, b, y, d, x) for a, b, d in map(flipped, range(1, 8))]
    partners += [(zh, zl, 1 - y, c, x), (zh, zl, y, c, 1 - x)]
    for partner in partners:
        pl.semaphore_signal(barrier, inc=1, device_id=partner, device_id_type=MESH)
    pl.semaphore_wait(barrier, len(partners))

    me = place(zh, zl, y, c)
    wcopies = {}

    def start_weights(f):
        a, b, d = flipped(f)
        slab = (b * 2 + d) * cols
        out = []
        for t in range(3):
            src = weights[t].at[:, pl.ds(pl.multiple_of(slab, 128), cols)]
            dst = gw_ref.at[me, :, pl.ds(t * cols, cols)]
            if f == 0:
                cp = pltpu.make_async_copy(src, dst, wr.at[f, t])
            else:
                cp = pltpu.make_async_remote_copy(
                    src_ref=src,
                    dst_ref=dst,
                    send_sem=ws.at[f, t],
                    recv_sem=wr.at[f, t],
                    device_id=(a, b, y, d, x),
                    device_id_type=MESH,
                )
            cp.start()
            out.append(cp)
        wcopies[f] = out

    ycopies = []

    def forward(f):
        for cp in wcopies[f]:
            if f == 0:
                cp.wait()
            else:
                cp.wait_recv()
        a, b, d = flipped(f)
        slot = place(a, b, y, d)
        cp = pltpu.make_async_remote_copy(
            src_ref=gw_ref.at[slot],
            dst_ref=gw_ref.at[slot],
            send_sem=ys.at[f],
            recv_sem=yr.at[f],
            device_id=(zh, zl, 1 - y, c, x),
            device_id_type=MESH,
        )
        cp.start()
        ycopies.append(cp)

    acopies = {}

    def start_tokens(k, src, slot, target):
        cp = pltpu.make_async_remote_copy(
            src_ref=src,
            dst_ref=ga_ref.at[slot],
            send_sem=as_.at[k],
            recv_sem=ar.at[k],
            device_id=target,
            device_id_type=MESH,
        )
        cp.start()
        acopies[k] = cp

    def token_slot(b, d, e):
        return (b * 2 + d) * 2 + e

    to_z, to_x, to_c = (zh, 1 - zl, y, c, x), (zh, zl, y, c, 1 - x), (zh, zl, y, 1 - c, x)
    mine = token_slot(zl, c, x)
    start_tokens(0, m_ref, mine, to_z)
    start_weights(0)
    start_weights(1)
    start_weights(4)
    start_tokens(1, m_ref, mine, to_x)
    start_tokens(2, m_ref, mine, to_c)
    local = pltpu.make_async_copy(m_ref, ga_ref.at[mine], ls.at[0])
    local.start()
    start_weights(5)
    forward(0)
    forward(1)
    acopies[0].wait_recv()
    theirs = token_slot(1 - zl, c, x)
    start_tokens(3, ga_ref.at[theirs], theirs, to_x)
    start_tokens(4, ga_ref.at[theirs], theirs, to_c)
    start_weights(2)
    forward(4)
    start_weights(6)
    start_weights(3)
    acopies[1].wait_recv()
    across = token_slot(zl, c, 1 - x)
    start_tokens(5, ga_ref.at[across], across, to_c)
    forward(2)
    forward(5)
    start_weights(7)
    acopies[3].wait_recv()
    far = token_slot(1 - zl, c, 1 - x)
    start_tokens(6, ga_ref.at[far], far, to_c)
    forward(3)
    forward(6)
    forward(7)
    local.wait()
    for k in (2, 4, 5, 6):
        acopies[k].wait_recv()
    for cp in ycopies:
        cp.wait_recv()
    for f in range(1, 8):
        for cp in wcopies[f]:
            cp.wait_send()
    for cp in ycopies:
        cp.wait_send()
    for k in range(7):
        acopies[k].wait_send()


def gather_operands(w_query, w_key, w_value, modulated):
    rows, half = w_query.shape
    tokens, width = modulated.shape
    dma = pltpu.SemaphoreType.DMA
    anywhere = pl.BlockSpec(memory_space=pl.ANY)
    gw, ga = pl.pallas_call(
        gather_kernel,
        out_shape=(
            jax.ShapeDtypeStruct((16, rows, 3 * half // 4), w_query.dtype),
            jax.ShapeDtypeStruct((8, tokens, width), modulated.dtype),
        ),
        in_specs=[anywhere] * 4,
        out_specs=(anywhere, anywhere),
        scratch_shapes=[dma((8, 3)), dma((8, 3)), dma((8,)), dma((8,)), dma((7,)), dma((7,)), dma((1,))],
        compiler_params=pltpu.CompilerParams(collective_id=0, has_side_effects=True),
        cost_estimate=pl.CostEstimate(flops=0, bytes_accessed=400_000_000, transcendentals=0),
    )(w_query, w_key, w_value, modulated)
    return gw.reshape(16 * rows, 3 * half // 4), ga.reshape(8 * tokens, width)


def attend_kernel(
    mask_ref, q_ref, k_ref, v_ref, kp_ref, vp_ref, ke_ref, ve_ref, kc_ref, vc_ref, o_ref, *, scale, tile, qtiles, ktiles
):
    g, h = pl.program_id(0), pl.program_id(1)
    own = g % 2 == 1
    k_prev = jnp.where(own, kp_ref[...], ke_ref[...])
    v_prev = jnp.where(own, vp_ref[...], ve_ref[...])
    keys = jnp.concatenate([kc_ref[...], k_prev, k_ref[...]], axis=0)
    vals = jnp.concatenate([vc_ref[...], v_prev, v_ref[...]], axis=0)
    for i in range(qtiles):
        q = q_ref[i * tile : (i + 1) * tile, :]
        s = lax.dot_general(q, keys, (((1,), (1,)), ((), ())), preferred_element_type=jnp.float32) * scale
        parts = []
        for j in range(ktiles):
            seen = mask_ref[((g * pl.num_programs(1) + h) * qtiles + i) * ktiles + j]
            parts.append(jnp.where(seen > 0, s[:, j * tile : (j + 1) * tile], -jnp.inf))
        s = jnp.concatenate(parts, axis=1)
        peak = jnp.max(s, axis=-1, keepdims=True)
        w = jnp.exp(s - peak)
        total = jnp.sum(w, axis=-1, keepdims=True)
        summed = jnp.dot(w.astype(jnp.bfloat16), vals, preferred_element_type=jnp.float32)
        o_ref[i * tile : (i + 1) * tile, :] = (summed / total).astype(jnp.bfloat16)


def attend(mask, q, k, v, k_edge, v_edge, k_cache, v_cache, scale, rows, head, qtiles, ktiles):
    groups, heads = q.shape[0] // rows, q.shape[1] // head
    cur = pl.BlockSpec((rows, head), lambda g, h: (g, h))
    prev = pl.BlockSpec((rows, head), lambda g, h: (jnp.maximum(g - 1, 0), h))
    edge = pl.BlockSpec((rows, head), lambda g, h: (g // 2, h))
    cache = pl.BlockSpec((rows, head), lambda g, h: (0, h))
    return pl.pallas_call(
        functools.partial(attend_kernel, scale=scale, tile=rows // qtiles, qtiles=qtiles, ktiles=ktiles),
        grid=(groups, heads),
        out_shape=jax.ShapeDtypeStruct(q.shape, jnp.bfloat16),
        in_specs=[pl.BlockSpec(memory_space=pltpu.SMEM), cur, cur, cur, prev, prev, edge, edge, cache, cache],
        out_specs=cur,
    )(mask, q, k, v, k, v, k_edge, v_edge, k_cache, v_cache)


def local_split(
    latents,
    timesteps,
    mod_shift,
    mod_scale,
    w_query,
    w_key,
    w_value,
    query_gain,
    key_gain,
    cache_keys,
    cache_values,
    owners,
    tile_mask,
):
    zh, zl, y, c, x = (lax.axis_index(a) for a in AXES)
    member = ((zh * 2 + zl) * 2 + y) * 2 + c
    modulated = modulate(latents, timesteps[0], mod_shift, mod_scale)
    root = owners[owners.shape[0] - 1]
    kept = jnp.where(member == root, jnp.concatenate([cache_keys, cache_values], axis=1), 0)
    cached = lax.psum(kept.astype(jnp.bfloat16), ("zh", "zl", "y", "c"))
    joined, tokens = gather_operands(w_query, w_key, w_value, modulated)
    half = w_query.shape[1]
    cols = half // 4
    slab = (zl * 2 + c) * cols
    projected = jnp.dot(tokens, joined, preferred_element_type=jnp.float32)
    raw_query = projected[:, :cols]
    raw_key = projected[:, cols : 2 * cols]
    raw_value = projected[:, 2 * cols :]
    squares = lax.psum(
        jnp.stack([jnp.sum(raw_query * raw_query, axis=1), jnp.sum(raw_key * raw_key, axis=1)]),
        ("zl", "c", "x"),
    )
    width = 2 * half
    q_gain = lax.dynamic_slice_in_dim(query_gain, slab, cols, 0)
    k_gain = lax.dynamic_slice_in_dim(key_gain, slab, cols, 0)
    query_rows = scaled_rows(raw_query, squares[0], width, q_gain)
    key_rows = scaled_rows(raw_key, squares[1], width, k_gain)
    value_rows = raw_value.astype(jnp.bfloat16)
    rows = query_rows.shape[0] // 4
    tails = [jnp.concatenate([a[s * rows : (s + 1) * rows] for a in (key_rows, value_rows)], axis=1) for s in (1, 3)]
    swapped = lax.ppermute(tails[0], "y", [(0, 1), (1, 0)])
    shifted = lax.ppermute(tails[1], ("zh", "y"), [(0, 1), (1, 2), (2, 3)])
    edges = jnp.concatenate(
        [jnp.where(y == 0, shifted, swapped), jnp.where(y == 0, swapped, shifted)], axis=0
    )
    heads = tile_mask.shape[0] // 4
    query_tiles, key_tiles = tile_mask.shape[1:]
    head = cols // heads
    mask = lax.dynamic_slice_in_dim(tile_mask, (zl * 2 + c) * heads, heads, 0)
    slots = jnp.arange(4)
    group_ids = ((zh * 2 + slots // 2) * 2 + y) * 2 + slots % 2
    tile_ids = jnp.arange(key_tiles)
    earlier = (tile_ids >= query_tiles) & (tile_ids < 2 * query_tiles)
    allowed = jnp.where(
        (group_ids == 0)[:, None, None, None] & earlier[None, None, None, :], 0, mask[None]
    ).reshape(-1)
    attended = attend(
        allowed,
        query_rows,
        key_rows,
        value_rows,
        edges[:, :cols],
        edges[:, cols:],
        lax.dynamic_slice_in_dim(cached, slab, cols, 1),
        lax.dynamic_slice_in_dim(cached, half + slab, cols, 1),
        1.0 / math.sqrt(head),
        rows,
        head,
        query_tiles,
        key_tiles,
    )
    out = lax.all_to_all(attended.reshape(4, rows, cols), ("zl", "c"), split_axis=0, concat_axis=2, tiled=True)
    return out.reshape(rows, half)


def solution(mesh):
    body, group, tok = local, "group", "tok"
    if mesh.shape["group"] == 16 and mesh.shape["tok"] == 2:
        mesh = jax.sharding.Mesh(mesh.devices.reshape(2, 2, 2, 2, 2), AXES)
        body, group, tok = local_split, ("zh", "zl", "y", "c"), "x"
    both = (*group, tok) if body is local_split else (group, tok)
    return jax.shard_map(
        body,
        mesh=mesh,
        in_specs=(
            P(both, None),
            P(group),
            P(),
            P(),
            P(group, tok),
            P(group, tok),
            P(group, tok),
            P(tok),
            P(tok),
            P(group, tok),
            P(group, tok),
            P(),
            P(tok, None, None),
        ),
        out_specs=P(group, tok),
        check_vma=False,
    )
```

```python
import functools
import math

import jax
import jax.numpy as jnp
from jax import lax
from jax.experimental import pallas as pl
from jax.experimental.pallas import tpu as pltpu
from jax.sharding import PartitionSpec as P

EPSILON = 1e-06
MESH = pl.DeviceIdType.MESH


def from_behind(block, axis, distance):
    devices = range(lax.axis_size(axis))
    route = [(i - distance, i) for i in devices if i - distance in devices]
    return lax.ppermute(block, axis, route)


def spread_2(value, axis, source):
    kept = jnp.where(lax.axis_index(axis) == source, value, 0).astype(value.dtype)
    return lax.psum(kept, axis)


def modulate(rows_block, timestep, mod_shift, mod_scale):
    values = rows_block.astype(jnp.float32)
    width = values.shape[-1]
    centred = values - jnp.mean(values, axis=-1, keepdims=True)
    spread = jnp.mean(centred * centred, axis=-1, keepdims=True)
    normed = centred * lax.rsqrt(spread + EPSILON)
    freqs = jnp.exp(-math.log(10000.0) * jnp.arange(width, dtype=jnp.float32) / width)
    angles = timestep.astype(jnp.float32) * freqs
    return (
        normed * (1.0 + mod_scale + 0.5 * jnp.cos(angles)) + mod_shift + 0.5 * jnp.sin(angles)
    ).astype(jnp.bfloat16)


def scaled_rows(raw, squares, width, gain):
    return (raw * lax.rsqrt(squares / width + EPSILON)[:, None] * gain).astype(jnp.bfloat16)


def dense_attention(query_heads, key_heads, value_heads, allowed, tile_rows, score_scale):
    group_rows = query_heads.shape[1]
    block_rows = 512 if group_rows % 512 == 0 else group_rows
    block_count = group_rows // block_rows
    tiles_per_block = block_rows // tile_rows

    def one_head(operands):
        query_head, key_head, value_head, head_mask = operands
        key_mask = jnp.repeat(head_mask, tile_rows, axis=1)

        def one_block(block_index):
            block_queries = lax.dynamic_slice_in_dim(
                query_head, block_index * block_rows, block_rows, 0
            )
            block_mask = lax.dynamic_slice_in_dim(
                key_mask, block_index * tiles_per_block, tiles_per_block, 0
            )
            row_mask = jnp.repeat(block_mask, tile_rows, axis=0)
            scores = (
                jnp.einsum("id,jd->ij", block_queries, key_head, preferred_element_type=jnp.float32)
                * score_scale
            )
            scores = jnp.where(row_mask > 0, scores, -jnp.inf)
            peak = jnp.max(scores, axis=-1, keepdims=True)
            weights = jnp.exp(scores - peak)
            summed = jnp.dot(
                weights.astype(jnp.bfloat16), value_head, preferred_element_type=jnp.float32
            )
            return (summed / jnp.sum(weights, axis=-1, keepdims=True)).astype(jnp.bfloat16)

        blocks_out = lax.map(one_block, jnp.arange(block_count, dtype=jnp.int32))
        return blocks_out.reshape(group_rows, query_head.shape[1])

    return lax.map(one_head, (query_heads, key_heads, value_heads, allowed))


def local(
    latents,
    timesteps,
    mod_shift,
    mod_scale,
    w_query,
    w_key,
    w_value,
    query_gain,
    key_gain,
    cache_keys,
    cache_values,
    owners,
    tile_mask,
):
    modulated = modulate(latents, timesteps[0], mod_shift, mod_scale)
    root = owners[owners.shape[0] - 1]
    head_cols = w_query.shape[1]
    slabs = (
        lax.all_gather(w_query, "group", axis=0, tiled=True),
        lax.all_gather(w_key, "group", axis=0, tiled=True),
        lax.all_gather(w_value, "group", axis=0, tiled=True),
    )
    joined = jnp.concatenate(slabs, axis=1)
    projected = jnp.dot(
        lax.all_gather(modulated, "tok", axis=0, tiled=True),
        joined,
        preferred_element_type=jnp.float32,
    )
    raw_query = projected[:, :head_cols]
    raw_key = projected[:, head_cols : 2 * head_cols]
    raw_value = projected[:, 2 * head_cols :]
    query_squares, key_squares = lax.psum(
        (jnp.sum(raw_query * raw_query, axis=1), jnp.sum(raw_key * raw_key, axis=1)), "tok"
    )
    width = head_cols * lax.axis_size("tok")
    query_rows = scaled_rows(raw_query, query_squares, width, query_gain)
    key_rows = scaled_rows(raw_key, key_squares, width, key_gain)
    value_rows = raw_value.astype(jnp.bfloat16)
    earlier_keys, earlier_values = from_behind((key_rows, value_rows), "group", 1)
    cached = (spread_2(cache_keys, "group", root), spread_2(cache_values, "group", root))
    group_rows = query_rows.shape[0]
    local_heads = tile_mask.shape[0]
    query_tiles = tile_mask.shape[1]
    key_tile_count = tile_mask.shape[2]
    tile_rows = group_rows // query_tiles
    head_size = head_cols // local_heads
    score_scale = 1.0 / math.sqrt(head_size)
    context_keys = jnp.concatenate([cached[0], earlier_keys, key_rows], axis=0)
    context_values = jnp.concatenate([cached[1], earlier_values, value_rows], axis=0)
    is_first = lax.axis_index("group") == 0
    tile_ids = jnp.arange(key_tile_count, dtype=jnp.int32)
    earlier_region = (tile_ids >= query_tiles) & (tile_ids < 2 * query_tiles)
    allowed = jnp.where(earlier_region[None, None, :] & is_first, 0, tile_mask)
    query_heads = query_rows.reshape(group_rows, local_heads, head_size).transpose(1, 0, 2)
    key_heads = context_keys.reshape(3 * group_rows, local_heads, head_size).transpose(1, 0, 2)
    value_heads = context_values.reshape(3 * group_rows, local_heads, head_size).transpose(1, 0, 2)
    attended = dense_attention(query_heads, key_heads, value_heads, allowed, tile_rows, score_scale)
    return attended.transpose(1, 0, 2).reshape(group_rows, head_cols)


AXES = ("zh", "zl", "y", "c", "x")


def gather_kernel(
    wq_ref, wk_ref, wv_ref, m_ref, ck_ref, cv_ref, flag_ref, gw_ref, ga_ref, cache_ref,
    kept, from_c, halves, from_z, part, from_y, from_zh, ws, wr, ys, yr, as_, ar, ls, cs, cr
):
    zh, zl, y, c, x = (lax.axis_index(a) for a in AXES)
    weights = (wq_ref, wk_ref, wv_ref)
    rows = wq_ref.shape[0]
    cols = gw_ref.shape[2] // 3

    def flipped(f):
        return (
            1 - zh if f & 4 else zh,
            1 - zl if f & 2 else zl,
            1 - c if f & 1 else c,
        )

    def place(fzh, fzl, fy, fc):
        return ((fzh * 2 + fzl) * 2 + fy) * 2 + fc

    barrier = pltpu.get_barrier_semaphore()
    partners = [(a, b, y, d, x) for a, b, d in map(flipped, range(1, 8))]
    partners += [(zh, zl, 1 - y, c, x), (zh, zl, y, c, 1 - x)]
    for partner in partners:
        pl.semaphore_signal(barrier, inc=1, device_id=partner, device_id_type=MESH)
    pl.semaphore_wait(barrier, len(partners))

    me = place(zh, zl, y, c)
    wcopies = {}

    def start_weights(f):
        a, b, d = flipped(f)
        slab = (b * 2 + d) * cols
        out = []
        for t in range(3):
            src = weights[t].at[:, pl.ds(pl.multiple_of(slab, 128), cols)]
            dst = gw_ref.at[me, :, pl.ds(t * cols, cols)]
            if f == 0:
                cp = pltpu.make_async_copy(src, dst, wr.at[f, t])
            else:
                cp = pltpu.make_async_remote_copy(
                    src_ref=src,
                    dst_ref=dst,
                    send_sem=ws.at[f, t],
                    recv_sem=wr.at[f, t],
                    device_id=(a, b, y, d, x),
                    device_id_type=MESH,
                )
            cp.start()
            out.append(cp)
        wcopies[f] = out

    ycopies = []

    def forward(f):
        for cp in wcopies[f]:
            if f == 0:
                cp.wait()
            else:
                cp.wait_recv()
        a, b, d = flipped(f)
        slot = place(a, b, y, d)
        cp = pltpu.make_async_remote_copy(
            src_ref=gw_ref.at[slot],
            dst_ref=gw_ref.at[slot],
            send_sem=ys.at[f],
            recv_sem=yr.at[f],
            device_id=(zh, zl, 1 - y, c, x),
            device_id_type=MESH,
        )
        cp.start()
        ycopies.append(cp)

    acopies = {}

    def start_tokens(k, src, slot, target):
        cp = pltpu.make_async_remote_copy(
            src_ref=src,
            dst_ref=ga_ref.at[slot],
            send_sem=as_.at[k],
            recv_sem=ar.at[k],
            device_id=target,
            device_id_type=MESH,
        )
        cp.start()
        acopies[k] = cp

    def token_slot(b, d, e):
        return (b * 2 + d) * 2 + e

    def start_cache(k, src, dst, target):
        cp = pltpu.make_async_remote_copy(
            src_ref=src,
            dst_ref=dst,
            send_sem=cs.at[k],
            recv_sem=cr.at[k],
            device_id=target,
            device_id_type=MESH,
        )
        cp.start()
        return cp

    to_z, to_x, to_c = (zh, 1 - zl, y, c, x), (zh, zl, y, c, 1 - x), (zh, zl, y, 1 - c, x)
    mine = token_slot(zl, c, x)
    start_tokens(0, m_ref, mine, to_z)
    start_weights(0)
    start_weights(1)
    start_weights(4)
    start_tokens(1, m_ref, mine, to_x)
    start_tokens(2, m_ref, mine, to_c)
    local = pltpu.make_async_copy(m_ref, ga_ref.at[mine], ls.at[0])
    local.start()
    start_weights(5)
    forward(0)
    for p in range(4):
        for t, ref in enumerate((ck_ref, cv_ref)):
            block = ref[:, p * cols : (p + 1) * cols].astype(jnp.float32) * flag_ref[...]
            kept[p, :, t * cols : (t + 1) * cols] = block.astype(jnp.bfloat16)
    cache_c = [start_cache(j, kept.at[2 * j + 1 - c], from_c.at[j], to_c) for j in range(2)]
    forward(1)
    for j in range(2):
        cache_c[j].wait()
        halves[j] = kept[2 * j + c] + from_c[j]
    cache_z = start_cache(2, halves.at[1 - zl], from_z, to_z)
    acopies[0].wait_recv()
    theirs = token_slot(1 - zl, c, x)
    start_tokens(3, ga_ref.at[theirs], theirs, to_x)
    start_tokens(4, ga_ref.at[theirs], theirs, to_c)
    start_weights(2)
    forward(4)
    cache_z.wait()
    part[0] = halves[zl] + from_z[...]
    cache_y = start_cache(3, part.at[0], from_y, (zh, zl, 1 - y, c, x))
    start_weights(6)
    start_weights(3)
    acopies[1].wait_recv()
    across = token_slot(zl, c, 1 - x)
    start_tokens(5, ga_ref.at[across], across, to_c)
    forward(2)
    forward(5)
    start_weights(7)
    cache_y.wait()
    part[1] = part[0] + from_y[...]
    cache_zh = start_cache(4, part.at[1], from_zh, (1 - zh, zl, y, c, x))
    acopies[3].wait_recv()
    far = token_slot(1 - zl, c, 1 - x)
    start_tokens(6, ga_ref.at[far], far, to_c)
    forward(3)
    forward(6)
    forward(7)
    cache_zh.wait()
    cache_ref[...] = part[1] + from_zh[...]
    local.wait()
    for k in (2, 4, 5, 6):
        acopies[k].wait_recv()
    for cp in ycopies:
        cp.wait_recv()
    for f in range(1, 8):
        for cp in wcopies[f]:
            cp.wait_send()
    for cp in ycopies:
        cp.wait_send()
    for k in range(7):
        acopies[k].wait_send()


def gather_operands(w_query, w_key, w_value, modulated, cache_keys, cache_values, flag):
    rows, half = w_query.shape
    tokens, width = modulated.shape
    dma = pltpu.SemaphoreType.DMA
    anywhere = pl.BlockSpec(memory_space=pl.ANY)
    vmem = pl.BlockSpec(memory_space=pltpu.VMEM)
    slab = (cache_keys.shape[0], half // 2)
    bf16 = jnp.bfloat16
    gw, ga, cached = pl.pallas_call(
        gather_kernel,
        out_shape=(
            jax.ShapeDtypeStruct((16, rows, 3 * half // 4), w_query.dtype),
            jax.ShapeDtypeStruct((8, tokens, width), modulated.dtype),
            jax.ShapeDtypeStruct(slab, bf16),
        ),
        in_specs=[anywhere] * 4 + [vmem] * 3,
        out_specs=(anywhere, anywhere, vmem),
        scratch_shapes=[
            pltpu.VMEM((4, *slab), bf16),
            pltpu.VMEM((2, *slab), bf16),
            pltpu.VMEM((2, *slab), bf16),
            pltpu.VMEM(slab, bf16),
            pltpu.VMEM((2, *slab), bf16),
            pltpu.VMEM(slab, bf16),
            pltpu.VMEM(slab, bf16),
            dma((8, 3)),
            dma((8, 3)),
            dma((8,)),
            dma((8,)),
            dma((7,)),
            dma((7,)),
            dma((1,)),
            dma((5,)),
            dma((5,)),
        ],
        compiler_params=pltpu.CompilerParams(
            collective_id=0, has_side_effects=True, vmem_limit_bytes=32 * 1024 * 1024
        ),
        cost_estimate=pl.CostEstimate(flops=0, bytes_accessed=400_000_000, transcendentals=0),
    )(w_query, w_key, w_value, modulated, cache_keys, cache_values, flag)
    return gw.reshape(16 * rows, 3 * half // 4), ga.reshape(8 * tokens, width), cached


def attend_kernel(
    mask_ref, q_ref, k_ref, v_ref, kp_ref, vp_ref, ke_ref, ve_ref, kc_ref, vc_ref, o_ref, *, scale, tile, qtiles, ktiles
):
    g, h = pl.program_id(0), pl.program_id(1)
    own = g % 2 == 1
    k_prev = jnp.where(own, kp_ref[...], ke_ref[...])
    v_prev = jnp.where(own, vp_ref[...], ve_ref[...])
    keys = jnp.concatenate([kc_ref[...], k_prev, k_ref[...]], axis=0)
    vals = jnp.concatenate([vc_ref[...], v_prev, v_ref[...]], axis=0)
    for i in range(qtiles):
        q = q_ref[i * tile : (i + 1) * tile, :]
        s = lax.dot_general(q, keys, (((1,), (1,)), ((), ())), preferred_element_type=jnp.float32) * scale
        parts = []
        for j in range(ktiles):
            seen = mask_ref[((g * pl.num_programs(1) + h) * qtiles + i) * ktiles + j]
            parts.append(jnp.where(seen > 0, s[:, j * tile : (j + 1) * tile], -jnp.inf))
        s = jnp.concatenate(parts, axis=1)
        peak = jnp.max(s, axis=-1, keepdims=True)
        w = jnp.exp(s - peak)
        total = jnp.sum(w, axis=-1, keepdims=True)
        summed = jnp.dot(w.astype(jnp.bfloat16), vals, preferred_element_type=jnp.float32)
        o_ref[i * tile : (i + 1) * tile, :] = (summed / total).astype(jnp.bfloat16)


def attend(mask, q, k, v, edges, cached, scale, rows, head, qtiles, ktiles):
    groups, heads = q.shape[0] // rows, q.shape[1] // head
    cur = pl.BlockSpec((rows, head), lambda g, h: (g, h))
    prev = pl.BlockSpec((rows, head), lambda g, h: (jnp.maximum(g - 1, 0), h))
    edge = [pl.BlockSpec((rows, head), lambda g, h, t=t: (g // 2, t * heads + h)) for t in range(2)]
    cache = [pl.BlockSpec((rows, head), lambda g, h, t=t: (0, t * heads + h)) for t in range(2)]
    return pl.pallas_call(
        functools.partial(attend_kernel, scale=scale, tile=rows // qtiles, qtiles=qtiles, ktiles=ktiles),
        grid=(groups, heads),
        out_shape=jax.ShapeDtypeStruct(q.shape, jnp.bfloat16),
        in_specs=[pl.BlockSpec(memory_space=pltpu.SMEM), cur, cur, cur, prev, prev, *edge, *cache],
        out_specs=cur,
    )(mask, q, k, v, k, v, edges, edges, cached, cached)


def local_split(
    latents,
    timesteps,
    mod_shift,
    mod_scale,
    w_query,
    w_key,
    w_value,
    query_gain,
    key_gain,
    cache_keys,
    cache_values,
    owners,
    tile_mask,
):
    zh, zl, y, c, x = (lax.axis_index(a) for a in AXES)
    member = ((zh * 2 + zl) * 2 + y) * 2 + c
    modulated = modulate(latents, timesteps[0], mod_shift, mod_scale)
    root = owners[owners.shape[0] - 1]
    half = w_query.shape[1]
    cols = half // 4
    flag = jnp.full((1, cols), member == root, jnp.float32)
    joined, tokens, cached = gather_operands(
        w_query, w_key, w_value, modulated, cache_keys, cache_values, flag
    )
    slab = (zl * 2 + c) * cols
    projected = jnp.dot(tokens, joined, preferred_element_type=jnp.float32)
    raw_query = projected[:, :cols]
    raw_key = projected[:, cols : 2 * cols]
    raw_value = projected[:, 2 * cols :]
    squares = lax.psum(
        jnp.stack([jnp.sum(raw_query * raw_query, axis=1), jnp.sum(raw_key * raw_key, axis=1)]),
        ("zl", "c", "x"),
    )
    width = 2 * half
    q_gain = lax.dynamic_slice_in_dim(query_gain, slab, cols, 0)
    k_gain = lax.dynamic_slice_in_dim(key_gain, slab, cols, 0)
    query_rows = scaled_rows(raw_query, squares[0], width, q_gain)
    key_rows = scaled_rows(raw_key, squares[1], width, k_gain)
    value_rows = raw_value.astype(jnp.bfloat16)
    rows = query_rows.shape[0] // 4
    tails = [jnp.concatenate([a[s * rows : (s + 1) * rows] for a in (key_rows, value_rows)], axis=1) for s in (1, 3)]
    swapped = lax.ppermute(tails[0], "y", [(0, 1), (1, 0)])
    shifted = lax.ppermute(tails[1], ("zh", "y"), [(0, 1), (1, 2), (2, 3)])
    edges = jnp.concatenate(
        [jnp.where(y == 0, shifted, swapped), jnp.where(y == 0, swapped, shifted)], axis=0
    )
    heads = tile_mask.shape[0] // 4
    query_tiles, key_tiles = tile_mask.shape[1:]
    head = cols // heads
    mask = lax.dynamic_slice_in_dim(tile_mask, (zl * 2 + c) * heads, heads, 0)
    slots = jnp.arange(4)
    group_ids = ((zh * 2 + slots // 2) * 2 + y) * 2 + slots % 2
    tile_ids = jnp.arange(key_tiles)
    earlier = (tile_ids >= query_tiles) & (tile_ids < 2 * query_tiles)
    allowed = jnp.where(
        (group_ids == 0)[:, None, None, None] & earlier[None, None, None, :], 0, mask[None]
    ).reshape(-1)
    attended = attend(
        allowed,
        query_rows,
        key_rows,
        value_rows,
        edges,
        cached,
        1.0 / math.sqrt(head),
        rows,
        head,
        query_tiles,
        key_tiles,
    )
    out = lax.all_to_all(attended.reshape(4, rows, cols), ("zl", "c"), split_axis=0, concat_axis=2, tiled=True)
    return out.reshape(rows, half)


def solution(mesh):
    body, group, tok = local, "group", "tok"
    if mesh.shape["group"] == 16 and mesh.shape["tok"] == 2:
        mesh = jax.sharding.Mesh(mesh.devices.reshape(2, 2, 2, 2, 2), AXES)
        body, group, tok = local_split, ("zh", "zl", "y", "c"), "x"
    both = (*group, tok) if body is local_split else (group, tok)
    return jax.shard_map(
        body,
        mesh=mesh,
        in_specs=(
            P(both, None),
            P(group),
            P(),
            P(),
            P(group, tok),
            P(group, tok),
            P(group, tok),
            P(tok),
            P(tok),
            P(group, tok),
            P(group, tok),
            P(),
            P(tok, None, None),
        ),
        out_specs=P(group, tok),
        check_vma=False,
    )
```

```python
import functools
import math

import jax
import jax.numpy as jnp
from jax import lax
from jax.experimental import pallas as pl
from jax.experimental.pallas import tpu as pltpu
from jax.sharding import PartitionSpec as P

EPSILON = 1e-06
MESH = pl.DeviceIdType.MESH


def from_behind(block, axis, distance):
    devices = range(lax.axis_size(axis))
    route = [(i - distance, i) for i in devices if i - distance in devices]
    return lax.ppermute(block, axis, route)


def spread_2(value, axis, source):
    kept = jnp.where(lax.axis_index(axis) == source, value, 0).astype(value.dtype)
    return lax.psum(kept, axis)


def modulate(rows_block, timestep, mod_shift, mod_scale):
    values = rows_block.astype(jnp.float32)
    width = values.shape[-1]
    centred = values - jnp.mean(values, axis=-1, keepdims=True)
    spread = jnp.mean(centred * centred, axis=-1, keepdims=True)
    normed = centred * lax.rsqrt(spread + EPSILON)
    freqs = jnp.exp(-math.log(10000.0) * jnp.arange(width, dtype=jnp.float32) / width)
    angles = timestep.astype(jnp.float32) * freqs
    return (
        normed * (1.0 + mod_scale + 0.5 * jnp.cos(angles)) + mod_shift + 0.5 * jnp.sin(angles)
    ).astype(jnp.bfloat16)


def scaled_rows(raw, squares, width, gain):
    return (raw * lax.rsqrt(squares / width + EPSILON)[:, None] * gain).astype(jnp.bfloat16)


def dense_attention(query_heads, key_heads, value_heads, allowed, tile_rows, score_scale):
    group_rows = query_heads.shape[1]
    block_rows = 512 if group_rows % 512 == 0 else group_rows
    block_count = group_rows // block_rows
    tiles_per_block = block_rows // tile_rows

    def one_head(operands):
        query_head, key_head, value_head, head_mask = operands
        key_mask = jnp.repeat(head_mask, tile_rows, axis=1)

        def one_block(block_index):
            block_queries = lax.dynamic_slice_in_dim(
                query_head, block_index * block_rows, block_rows, 0
            )
            block_mask = lax.dynamic_slice_in_dim(
                key_mask, block_index * tiles_per_block, tiles_per_block, 0
            )
            row_mask = jnp.repeat(block_mask, tile_rows, axis=0)
            scores = (
                jnp.einsum("id,jd->ij", block_queries, key_head, preferred_element_type=jnp.float32)
                * score_scale
            )
            scores = jnp.where(row_mask > 0, scores, -jnp.inf)
            peak = jnp.max(scores, axis=-1, keepdims=True)
            weights = jnp.exp(scores - peak)
            summed = jnp.dot(
                weights.astype(jnp.bfloat16), value_head, preferred_element_type=jnp.float32
            )
            return (summed / jnp.sum(weights, axis=-1, keepdims=True)).astype(jnp.bfloat16)

        blocks_out = lax.map(one_block, jnp.arange(block_count, dtype=jnp.int32))
        return blocks_out.reshape(group_rows, query_head.shape[1])

    return lax.map(one_head, (query_heads, key_heads, value_heads, allowed))


def local(
    latents,
    timesteps,
    mod_shift,
    mod_scale,
    w_query,
    w_key,
    w_value,
    query_gain,
    key_gain,
    cache_keys,
    cache_values,
    owners,
    tile_mask,
):
    modulated = modulate(latents, timesteps[0], mod_shift, mod_scale)
    root = owners[owners.shape[0] - 1]
    head_cols = w_query.shape[1]
    slabs = (
        lax.all_gather(w_query, "group", axis=0, tiled=True),
        lax.all_gather(w_key, "group", axis=0, tiled=True),
        lax.all_gather(w_value, "group", axis=0, tiled=True),
    )
    joined = jnp.concatenate(slabs, axis=1)
    projected = jnp.dot(
        lax.all_gather(modulated, "tok", axis=0, tiled=True),
        joined,
        preferred_element_type=jnp.float32,
    )
    raw_query = projected[:, :head_cols]
    raw_key = projected[:, head_cols : 2 * head_cols]
    raw_value = projected[:, 2 * head_cols :]
    query_squares, key_squares = lax.psum(
        (jnp.sum(raw_query * raw_query, axis=1), jnp.sum(raw_key * raw_key, axis=1)), "tok"
    )
    width = head_cols * lax.axis_size("tok")
    query_rows = scaled_rows(raw_query, query_squares, width, query_gain)
    key_rows = scaled_rows(raw_key, key_squares, width, key_gain)
    value_rows = raw_value.astype(jnp.bfloat16)
    earlier_keys, earlier_values = from_behind((key_rows, value_rows), "group", 1)
    cached = (spread_2(cache_keys, "group", root), spread_2(cache_values, "group", root))
    group_rows = query_rows.shape[0]
    local_heads = tile_mask.shape[0]
    query_tiles = tile_mask.shape[1]
    key_tile_count = tile_mask.shape[2]
    tile_rows = group_rows // query_tiles
    head_size = head_cols // local_heads
    score_scale = 1.0 / math.sqrt(head_size)
    context_keys = jnp.concatenate([cached[0], earlier_keys, key_rows], axis=0)
    context_values = jnp.concatenate([cached[1], earlier_values, value_rows], axis=0)
    is_first = lax.axis_index("group") == 0
    tile_ids = jnp.arange(key_tile_count, dtype=jnp.int32)
    earlier_region = (tile_ids >= query_tiles) & (tile_ids < 2 * query_tiles)
    allowed = jnp.where(earlier_region[None, None, :] & is_first, 0, tile_mask)
    query_heads = query_rows.reshape(group_rows, local_heads, head_size).transpose(1, 0, 2)
    key_heads = context_keys.reshape(3 * group_rows, local_heads, head_size).transpose(1, 0, 2)
    value_heads = context_values.reshape(3 * group_rows, local_heads, head_size).transpose(1, 0, 2)
    attended = dense_attention(query_heads, key_heads, value_heads, allowed, tile_rows, score_scale)
    return attended.transpose(1, 0, 2).reshape(group_rows, head_cols)


AXES = ("zh", "zl", "y", "c", "x")


def gather_kernel(
    wq_ref, wk_ref, wv_ref, m_ref, ck_ref, cv_ref, flag_ref, gw_ref, ga_ref, cache_ref,
    kept, from_c, halves, from_z, part, from_y, from_zh, ws, wr, ys, yr, as_, ar, ls, cs, cr
):
    zh, zl, y, c, x = (lax.axis_index(a) for a in AXES)
    weights = (wq_ref, wk_ref, wv_ref)
    rows = wq_ref.shape[0]
    cols = gw_ref.shape[2] // 3

    def flipped(f):
        return (
            1 - zh if f & 4 else zh,
            1 - zl if f & 2 else zl,
            1 - c if f & 1 else c,
        )

    def place(fzh, fzl, fy, fc):
        return ((fzh * 2 + fzl) * 2 + fy) * 2 + fc

    barrier = pltpu.get_barrier_semaphore()
    partners = [(a, b, y, d, x) for a, b, d in map(flipped, range(1, 8))]
    partners += [(zh, zl, 1 - y, c, x), (zh, zl, y, c, 1 - x)]
    for partner in partners:
        pl.semaphore_signal(barrier, inc=1, device_id=partner, device_id_type=MESH)
    pl.semaphore_wait(barrier, len(partners))

    me = place(zh, zl, y, c)
    wcopies = {}

    def start_weights(f):
        a, b, d = flipped(f)
        slab = (b * 2 + d) * cols
        out = []
        for t in range(3):
            src = weights[t].at[:, pl.ds(pl.multiple_of(slab, 128), cols)]
            dst = gw_ref.at[me, :, pl.ds(t * cols, cols)]
            if f == 0:
                cp = pltpu.make_async_copy(src, dst, wr.at[f, t])
            else:
                cp = pltpu.make_async_remote_copy(
                    src_ref=src,
                    dst_ref=dst,
                    send_sem=ws.at[f, t],
                    recv_sem=wr.at[f, t],
                    device_id=(a, b, y, d, x),
                    device_id_type=MESH,
                )
            cp.start()
            out.append(cp)
        wcopies[f] = out

    ycopies = []

    def forward(f):
        for cp in wcopies[f]:
            if f == 0:
                cp.wait()
            else:
                cp.wait_recv()
        a, b, d = flipped(f)
        slot = place(a, b, y, d)
        cp = pltpu.make_async_remote_copy(
            src_ref=gw_ref.at[slot],
            dst_ref=gw_ref.at[slot],
            send_sem=ys.at[f],
            recv_sem=yr.at[f],
            device_id=(zh, zl, 1 - y, c, x),
            device_id_type=MESH,
        )
        cp.start()
        ycopies.append(cp)

    acopies = {}

    def start_tokens(k, src, slot, target):
        cp = pltpu.make_async_remote_copy(
            src_ref=src,
            dst_ref=ga_ref.at[slot],
            send_sem=as_.at[k],
            recv_sem=ar.at[k],
            device_id=target,
            device_id_type=MESH,
        )
        cp.start()
        acopies[k] = cp

    def token_slot(b, d, e):
        return (b * 2 + d) * 2 + e

    def start_cache(k, src, dst, target):
        cp = pltpu.make_async_remote_copy(
            src_ref=src,
            dst_ref=dst,
            send_sem=cs.at[k],
            recv_sem=cr.at[k],
            device_id=target,
            device_id_type=MESH,
        )
        cp.start()
        return cp

    to_z, to_x, to_c = (zh, 1 - zl, y, c, x), (zh, zl, y, c, 1 - x), (zh, zl, y, 1 - c, x)
    mine = token_slot(zl, c, x)
    start_tokens(0, m_ref, mine, to_z)
    start_weights(0)
    start_weights(1)
    start_weights(4)
    start_tokens(1, m_ref, mine, to_x)
    start_tokens(2, m_ref, mine, to_c)
    local = pltpu.make_async_copy(m_ref, ga_ref.at[mine], ls.at[0])
    local.start()
    start_weights(5)
    forward(0)
    for p in range(4):
        for t, ref in enumerate((ck_ref, cv_ref)):
            block = ref[:, p * cols : (p + 1) * cols].astype(jnp.float32) * flag_ref[...]
            kept[p, :, t * cols : (t + 1) * cols] = block.astype(jnp.bfloat16)
    cache_c = [start_cache(j, kept.at[2 * j + 1 - c], from_c.at[j], to_c) for j in range(2)]
    forward(1)
    for j in range(2):
        cache_c[j].wait()
        halves[j] = kept[2 * j + c] + from_c[j]
    cache_z = start_cache(2, halves.at[1 - zl], from_z, to_z)
    acopies[0].wait_recv()
    theirs = token_slot(1 - zl, c, x)
    start_tokens(3, ga_ref.at[theirs], theirs, to_x)
    start_tokens(4, ga_ref.at[theirs], theirs, to_c)
    start_weights(2)
    forward(4)
    cache_z.wait()
    part[0] = halves[zl] + from_z[...]
    cache_y = start_cache(3, part.at[0], from_y, (zh, zl, 1 - y, c, x))
    start_weights(6)
    start_weights(3)
    acopies[1].wait_recv()
    across = token_slot(zl, c, 1 - x)
    start_tokens(5, ga_ref.at[across], across, to_c)
    forward(2)
    forward(5)
    start_weights(7)
    cache_y.wait()
    part[1] = part[0] + from_y[...]
    cache_zh = start_cache(4, part.at[1], from_zh, (1 - zh, zl, y, c, x))
    acopies[3].wait_recv()
    far = token_slot(1 - zl, c, 1 - x)
    start_tokens(6, ga_ref.at[far], far, to_c)
    forward(3)
    forward(6)
    forward(7)
    cache_zh.wait()
    cache_ref[...] = part[1] + from_zh[...]
    local.wait()
    for k in (2, 4, 5, 6):
        acopies[k].wait_recv()
    for cp in ycopies:
        cp.wait_recv()
    for f in range(1, 8):
        for cp in wcopies[f]:
            cp.wait_send()
    for cp in ycopies:
        cp.wait_send()
    for k in range(7):
        acopies[k].wait_send()


def gather_operands(w_query, w_key, w_value, modulated, cache_keys, cache_values, flag):
    rows, half = w_query.shape
    tokens, width = modulated.shape
    dma = pltpu.SemaphoreType.DMA
    anywhere = pl.BlockSpec(memory_space=pl.ANY)
    vmem = pl.BlockSpec(memory_space=pltpu.VMEM)
    slab = (cache_keys.shape[0], half // 2)
    bf16 = jnp.bfloat16
    gw, ga, cached = pl.pallas_call(
        gather_kernel,
        out_shape=(
            jax.ShapeDtypeStruct((16, rows, 3 * half // 4), w_query.dtype),
            jax.ShapeDtypeStruct((8, tokens, width), modulated.dtype),
            jax.ShapeDtypeStruct(slab, bf16),
        ),
        in_specs=[anywhere] * 4 + [vmem] * 3,
        out_specs=(anywhere, anywhere, vmem),
        scratch_shapes=[
            pltpu.VMEM((4, *slab), bf16),
            pltpu.VMEM((2, *slab), bf16),
            pltpu.VMEM((2, *slab), bf16),
            pltpu.VMEM(slab, bf16),
            pltpu.VMEM((2, *slab), bf16),
            pltpu.VMEM(slab, bf16),
            pltpu.VMEM(slab, bf16),
            dma((8, 3)),
            dma((8, 3)),
            dma((8,)),
            dma((8,)),
            dma((7,)),
            dma((7,)),
            dma((1,)),
            dma((5,)),
            dma((5,)),
        ],
        compiler_params=pltpu.CompilerParams(
            collective_id=0, has_side_effects=True, vmem_limit_bytes=32 * 1024 * 1024
        ),
        cost_estimate=pl.CostEstimate(flops=0, bytes_accessed=400_000_000, transcendentals=0),
    )(w_query, w_key, w_value, modulated, cache_keys, cache_values, flag)
    return gw.reshape(16 * rows, 3 * half // 4), ga.reshape(8 * tokens, width), cached


def tail_kernel(
    raw_ref, qg_ref, kg_ref, bias_ref, cache_ref, o_ref,
    q_s, k_all, v_all, att, sq, rx, qs, qr, es, er, os_, or_, *, scale, heads, width
):
    zh, zl, y, c, x = (lax.axis_index(a) for a in AXES)
    rows, cols = att.shape[1:]
    head = cols // heads
    tile = rows // 2
    y_here, y_there = (zh, zl, 1 - y, c, x), (1 - zh, zl, 1 - y, c, x)

    def flipped(f):
        return (zh, 1 - zl if f & 4 else zl, y, 1 - c if f & 2 else c, 1 - x if f & 1 else x)

    barrier = pltpu.get_barrier_semaphore()
    partners = [flipped(f) for f in range(1, 8)] + [y_here, y_there]
    for partner in partners:
        pl.semaphore_signal(barrier, inc=1, device_id=partner, device_id_type=MESH)

    for s in range(4):
        part = slice(s * rows, (s + 1) * rows)
        a, b = raw_ref[part, :cols], raw_ref[part, cols : 2 * cols]
        lanes = lax.broadcasted_iota(jnp.int32, (rows, 128), 1)
        both = jnp.where(
            lanes % 8 < 4,
            jnp.sum(a * a, axis=1, keepdims=True),
            jnp.sum(b * b, axis=1, keepdims=True),
        )
        sq[:, part] = both.T[:8]
    for s in range(4):
        v_all[s // 2 * 3 + 1 + s % 2] = raw_ref[s * rows : (s + 1) * rows, 2 * cols :].astype(jnp.bfloat16)
    pl.semaphore_wait(barrier, len(partners))

    copies = []
    for f in range(1, 8):
        cp = pltpu.make_async_remote_copy(
            src_ref=sq,
            dst_ref=rx.at[f],
            send_sem=qs.at[f],
            recv_sem=qr.at[f],
            device_id=flipped(f),
            device_id_type=MESH,
        )
        cp.start()
        copies.append(cp)

    onward = (zh + y - 2 * zh * y, zl, 1 - y, c, x)

    def start_edges(k, ref):
        out = []
        for t, (src, dst, target) in enumerate(((2, y, y_here), (5, 1 - y, onward))):
            cp = pltpu.make_async_remote_copy(
                src_ref=ref.at[src],
                dst_ref=ref.at[dst * 3],
                send_sem=es.at[k, t],
                recv_sem=er.at[k, t],
                device_id=target,
                device_id_type=MESH,
            )
            cp.start()
            out.append(cp)
        return out

    edges = start_edges(0, v_all)
    total = sq[...]
    for f in range(1, 8):
        copies[f - 1].wait_recv()
        total = total + rx[f]
    for s in range(4):
        part = slice(s * rows, (s + 1) * rows)
        sums = jnp.concatenate([total[:, part]] * 16, axis=0).T
        inverse = lax.rsqrt(sums / width + EPSILON)
        k_all[s // 2 * 3 + 1 + s % 2] = (
            raw_ref[part, cols : 2 * cols] * inverse[:, 4:5] * kg_ref[...]
        ).astype(jnp.bfloat16)
        q_s[s] = (raw_ref[part, :cols] * inverse[:, 0:1] * qg_ref[...]).astype(jnp.bfloat16)
    edges += start_edges(1, k_all)

    def attend(n, b, d):
        slot = b * 2 + d

        def one_head(h, carry):
            span = pl.ds(pl.multiple_of(h * head, head), head)
            behind = pl.ds(pl.multiple_of(cols + h * head, head), head)
            old_keys, old_values = cache_ref[:, span], cache_ref[:, behind]
            near_keys = k_all[pl.ds(b * 3 + d, 2), :, span].reshape(2 * rows, head)
            near_values = v_all[pl.ds(b * 3 + d, 2), :, span].reshape(2 * rows, head)
            keys = jnp.concatenate([old_keys, near_keys], axis=0)
            values = jnp.concatenate([old_values, near_values], axis=0)
            query = q_s[slot, :, span]
            for i in range(2):
                scores = lax.dot_general(
                    query[i * tile : (i + 1) * tile],
                    keys,
                    (((1,), (1,)), ((), ())),
                    preferred_element_type=jnp.float32,
                )
                scores = scores * scale + bias_ref[(slot * heads + h) * 2 + i]
                peak = jnp.max(scores, axis=-1, keepdims=True)
                weights = jnp.exp(scores - peak)
                summed = jnp.dot(weights.astype(jnp.bfloat16), values, preferred_element_type=jnp.float32)
                att[n, i * tile : (i + 1) * tile, span] = (
                    summed / jnp.sum(weights, axis=-1, keepdims=True)
                ).astype(jnp.bfloat16)
            return carry

        lax.fori_loop(0, heads, one_head, 0)

    me = zl * 2 + c

    def block(p):
        return o_ref.at[:, pl.ds(pl.multiple_of(p * cols, 128), cols)]

    def push(n, b, d):
        return pltpu.make_async_remote_copy(
            src_ref=att.at[n],
            dst_ref=block(me),
            send_sem=os_.at[n],
            recv_sem=or_.at[me],
            device_id=(zh, b, y, d, x),
            device_id_type=MESH,
        )

    order = [(0, 1 - zl, 1), (1, zl, 1), (2, 1 - zl, 0), (3, zl, 0)]
    for n, b, d in order:
        if n == 2:
            for cp in edges:
                cp.wait_recv()
        attend(n, b, d)
        if n % 2 == 0:
            push(n, b, d).start()
        else:

            @pl.when(c == d)
            def _():
                o_ref[:, pl.ds(pl.multiple_of(me * cols, 128), cols)] = att[n]

            @pl.when(c != d)
            def _():
                push(n, b, d).start()

    for p in ((1 - zl) * 2 + c, zl * 2 + 1 - c, (1 - zl) * 2 + 1 - c):
        pltpu.make_async_remote_copy(
            src_ref=att.at[0],
            dst_ref=block(p),
            send_sem=os_.at[0],
            recv_sem=or_.at[p],
            device_id=flipped(4),
            device_id_type=MESH,
        ).wait_recv()
    for cp in copies + edges:
        cp.wait_send()
    for n, b, d in order:
        if n % 2 == 0:
            push(n, b, d).wait_send()
        else:

            @pl.when(c != d)
            def _():
                push(n, b, d).wait_send()


def attend_groups(raw, q_gain, k_gain, bias, cached, scale, heads, width):
    rows, cols = raw.shape[0] // 4, raw.shape[1] // 3
    dma = pltpu.SemaphoreType.DMA
    bf16 = jnp.bfloat16
    vmem = pl.BlockSpec(memory_space=pltpu.VMEM)
    return pl.pallas_call(
        functools.partial(tail_kernel, scale=scale, heads=heads, width=width),
        out_shape=jax.ShapeDtypeStruct((rows, 4 * cols), bf16),
        in_specs=[vmem] * 5,
        out_specs=vmem,
        scratch_shapes=[
            pltpu.VMEM((4, rows, cols), bf16),
            pltpu.VMEM((6, rows, cols), bf16),
            pltpu.VMEM((6, rows, cols), bf16),
            pltpu.VMEM((4, rows, cols), bf16),
            pltpu.VMEM((8, 4 * rows), jnp.float32),
            pltpu.VMEM((8, 8, 4 * rows), jnp.float32),
            dma((8,)),
            dma((8,)),
            dma((2, 2)),
            dma((2, 2)),
            dma((4,)),
            dma((4,)),
        ],
        compiler_params=pltpu.CompilerParams(
            collective_id=1, has_side_effects=True, vmem_limit_bytes=40 * 1024 * 1024
        ),
    )(raw, q_gain, k_gain, bias, cached)


def local_split(
    latents,
    timesteps,
    mod_shift,
    mod_scale,
    w_query,
    w_key,
    w_value,
    query_gain,
    key_gain,
    cache_keys,
    cache_values,
    owners,
    tile_mask,
):
    zh, zl, y, c, x = (lax.axis_index(a) for a in AXES)
    member = ((zh * 2 + zl) * 2 + y) * 2 + c
    modulated = modulate(latents, timesteps[0], mod_shift, mod_scale)
    root = owners[owners.shape[0] - 1]
    half = w_query.shape[1]
    cols = half // 4
    flag = jnp.full((1, cols), member == root, jnp.float32)
    joined, tokens, cached = gather_operands(
        w_query, w_key, w_value, modulated, cache_keys, cache_values, flag
    )
    slab = (zl * 2 + c) * cols
    projected = jnp.dot(tokens, joined, preferred_element_type=jnp.float32)
    q_gain = lax.dynamic_slice_in_dim(query_gain, slab, cols, 0)[None]
    k_gain = lax.dynamic_slice_in_dim(key_gain, slab, cols, 0)[None]
    heads = tile_mask.shape[0] // 4
    query_tiles, key_tiles = tile_mask.shape[1:]
    head = cols // heads
    mask = lax.dynamic_slice_in_dim(tile_mask, (zl * 2 + c) * heads, heads, 0)
    slots = jnp.arange(4)
    group_ids = ((zh * 2 + slots // 2) * 2 + y) * 2 + slots % 2
    tile_ids = jnp.arange(key_tiles)
    earlier = (tile_ids >= query_tiles) & (tile_ids < 2 * query_tiles)
    allowed = jnp.where(
        (group_ids == 0)[:, None, None, None] & earlier[None, None, None, :], 0, mask[None]
    )
    bias = jnp.repeat(jnp.where(allowed > 0, 0.0, -jnp.inf), latents.shape[0], axis=-1)
    bias = bias.reshape(4 * heads * query_tiles, 1, -1).astype(jnp.float32)
    return attend_groups(projected, q_gain, k_gain, bias, cached, 1.0 / math.sqrt(head), heads, 2 * half)


def solution(mesh):
    body, group, tok = local, "group", "tok"
    if mesh.shape["group"] == 16 and mesh.shape["tok"] == 2:
        mesh = jax.sharding.Mesh(mesh.devices.reshape(2, 2, 2, 2, 2), AXES)
        body, group, tok = local_split, ("zh", "zl", "y", "c"), "x"
    both = (*group, tok) if body is local_split else (group, tok)
    return jax.shard_map(
        body,
        mesh=mesh,
        in_specs=(
            P(both, None),
            P(group),
            P(),
            P(),
            P(group, tok),
            P(group, tok),
            P(group, tok),
            P(tok),
            P(tok),
            P(group, tok),
            P(group, tok),
            P(),
            P(tok, None, None),
        ),
        out_specs=P(group, tok),
        check_vma=False,
    )
```

```python
import functools
import math

import jax
import jax.numpy as jnp
from jax import lax
from jax.experimental import pallas as pl
from jax.experimental.pallas import tpu as pltpu
from jax.sharding import PartitionSpec as P

EPSILON = 1e-06
MESH = pl.DeviceIdType.MESH


def from_behind(block, axis, distance):
    devices = range(lax.axis_size(axis))
    route = [(i - distance, i) for i in devices if i - distance in devices]
    return lax.ppermute(block, axis, route)


def spread_2(value, axis, source):
    kept = jnp.where(lax.axis_index(axis) == source, value, 0).astype(value.dtype)
    return lax.psum(kept, axis)


def modulate(rows_block, timestep, mod_shift, mod_scale):
    values = rows_block.astype(jnp.float32)
    width = values.shape[-1]
    centred = values - jnp.mean(values, axis=-1, keepdims=True)
    spread = jnp.mean(centred * centred, axis=-1, keepdims=True)
    normed = centred * lax.rsqrt(spread + EPSILON)
    freqs = jnp.exp(-math.log(10000.0) * jnp.arange(width, dtype=jnp.float32) / width)
    angles = timestep.astype(jnp.float32) * freqs
    return (
        normed * (1.0 + mod_scale + 0.5 * jnp.cos(angles)) + mod_shift + 0.5 * jnp.sin(angles)
    ).astype(jnp.bfloat16)


def scaled_rows(raw, squares, width, gain):
    return (raw * lax.rsqrt(squares / width + EPSILON)[:, None] * gain).astype(jnp.bfloat16)


def dense_attention(query_heads, key_heads, value_heads, allowed, tile_rows, score_scale):
    group_rows = query_heads.shape[1]
    block_rows = 512 if group_rows % 512 == 0 else group_rows
    block_count = group_rows // block_rows
    tiles_per_block = block_rows // tile_rows

    def one_head(operands):
        query_head, key_head, value_head, head_mask = operands
        key_mask = jnp.repeat(head_mask, tile_rows, axis=1)

        def one_block(block_index):
            block_queries = lax.dynamic_slice_in_dim(
                query_head, block_index * block_rows, block_rows, 0
            )
            block_mask = lax.dynamic_slice_in_dim(
                key_mask, block_index * tiles_per_block, tiles_per_block, 0
            )
            row_mask = jnp.repeat(block_mask, tile_rows, axis=0)
            scores = (
                jnp.einsum("id,jd->ij", block_queries, key_head, preferred_element_type=jnp.float32)
                * score_scale
            )
            scores = jnp.where(row_mask > 0, scores, -jnp.inf)
            peak = jnp.max(scores, axis=-1, keepdims=True)
            weights = jnp.exp(scores - peak)
            summed = jnp.dot(
                weights.astype(jnp.bfloat16), value_head, preferred_element_type=jnp.float32
            )
            return (summed / jnp.sum(weights, axis=-1, keepdims=True)).astype(jnp.bfloat16)

        blocks_out = lax.map(one_block, jnp.arange(block_count, dtype=jnp.int32))
        return blocks_out.reshape(group_rows, query_head.shape[1])

    return lax.map(one_head, (query_heads, key_heads, value_heads, allowed))


def local(
    latents,
    timesteps,
    mod_shift,
    mod_scale,
    w_query,
    w_key,
    w_value,
    query_gain,
    key_gain,
    cache_keys,
    cache_values,
    owners,
    tile_mask,
):
    modulated = modulate(latents, timesteps[0], mod_shift, mod_scale)
    root = owners[owners.shape[0] - 1]
    head_cols = w_query.shape[1]
    slabs = (
        lax.all_gather(w_query, "group", axis=0, tiled=True),
        lax.all_gather(w_key, "group", axis=0, tiled=True),
        lax.all_gather(w_value, "group", axis=0, tiled=True),
    )
    joined = jnp.concatenate(slabs, axis=1)
    projected = jnp.dot(
        lax.all_gather(modulated, "tok", axis=0, tiled=True),
        joined,
        preferred_element_type=jnp.float32,
    )
    raw_query = projected[:, :head_cols]
    raw_key = projected[:, head_cols : 2 * head_cols]
    raw_value = projected[:, 2 * head_cols :]
    query_squares, key_squares = lax.psum(
        (jnp.sum(raw_query * raw_query, axis=1), jnp.sum(raw_key * raw_key, axis=1)), "tok"
    )
    width = head_cols * lax.axis_size("tok")
    query_rows = scaled_rows(raw_query, query_squares, width, query_gain)
    key_rows = scaled_rows(raw_key, key_squares, width, key_gain)
    value_rows = raw_value.astype(jnp.bfloat16)
    earlier_keys, earlier_values = from_behind((key_rows, value_rows), "group", 1)
    cached = (spread_2(cache_keys, "group", root), spread_2(cache_values, "group", root))
    group_rows = query_rows.shape[0]
    local_heads = tile_mask.shape[0]
    query_tiles = tile_mask.shape[1]
    key_tile_count = tile_mask.shape[2]
    tile_rows = group_rows // query_tiles
    head_size = head_cols // local_heads
    score_scale = 1.0 / math.sqrt(head_size)
    context_keys = jnp.concatenate([cached[0], earlier_keys, key_rows], axis=0)
    context_values = jnp.concatenate([cached[1], earlier_values, value_rows], axis=0)
    is_first = lax.axis_index("group") == 0
    tile_ids = jnp.arange(key_tile_count, dtype=jnp.int32)
    earlier_region = (tile_ids >= query_tiles) & (tile_ids < 2 * query_tiles)
    allowed = jnp.where(earlier_region[None, None, :] & is_first, 0, tile_mask)
    query_heads = query_rows.reshape(group_rows, local_heads, head_size).transpose(1, 0, 2)
    key_heads = context_keys.reshape(3 * group_rows, local_heads, head_size).transpose(1, 0, 2)
    value_heads = context_values.reshape(3 * group_rows, local_heads, head_size).transpose(1, 0, 2)
    attended = dense_attention(query_heads, key_heads, value_heads, allowed, tile_rows, score_scale)
    return attended.transpose(1, 0, 2).reshape(group_rows, head_cols)


AXES = ("zh", "zl", "y", "c", "x")


def gather_kernel(
    wq_ref, wk_ref, wv_ref, lat_ref, gain_ref, shift_ref, ck_ref, cv_ref, flag_ref, gw_ref, ga_ref, cache_ref,
    m_ref,    kept, from_c, halves, from_z, part, from_y, from_zh, ws, wr, ys, yr, as_, ar, ls, cs, cr
):
    zh, zl, y, c, x = (lax.axis_index(a) for a in AXES)
    weights = (wq_ref, wk_ref, wv_ref)
    rows = wq_ref.shape[0]
    cols = gw_ref.shape[2] // 3

    def flipped(f):
        return (
            1 - zh if f & 4 else zh,
            1 - zl if f & 2 else zl,
            1 - c if f & 1 else c,
        )

    def place(fzh, fzl, fy, fc):
        return ((fzh * 2 + fzl) * 2 + fy) * 2 + fc

    barrier = pltpu.get_barrier_semaphore()
    partners = [(a, b, y, d, x) for a, b, d in map(flipped, range(1, 8))]
    partners += [(zh, zl, 1 - y, c, x), (zh, zl, y, c, 1 - x)]
    for partner in partners:
        pl.semaphore_signal(barrier, inc=1, device_id=partner, device_id_type=MESH)
    pl.semaphore_wait(barrier, len(partners))

    me = place(zh, zl, y, c)
    wcopies = {}

    def start_weights(f, t):
        a, b, d = flipped(f)
        slab = (b * 2 + d) * cols
        src = weights[t].at[:, pl.ds(pl.multiple_of(slab, 128), cols)]
        dst = gw_ref.at[me, :, pl.ds(t * cols, cols)]
        if f == 0:
            cp = pltpu.make_async_copy(src, dst, wr.at[f, t])
        else:
            cp = pltpu.make_async_remote_copy(
                src_ref=src,
                dst_ref=dst,
                send_sem=ws.at[f, t],
                recv_sem=wr.at[f, t],
                device_id=(a, b, y, d, x),
                device_id_type=MESH,
            )
        cp.start()
        wcopies[f, t] = cp

    ycopies = []

    def forward(f, t):
        if f == 0:
            wcopies[f, t].wait()
        else:
            wcopies[f, t].wait_recv()
        a, b, d = flipped(f)
        piece = gw_ref.at[place(a, b, y, d), :, pl.ds(t * cols, cols)]
        cp = pltpu.make_async_remote_copy(
            src_ref=piece,
            dst_ref=piece,
            send_sem=ys.at[f, t],
            recv_sem=yr.at[f, t],
            device_id=(zh, zl, 1 - y, c, x),
            device_id_type=MESH,
        )
        cp.start()
        ycopies.append(cp)

    acopies = {}

    def start_tokens(k, src, slot, target):
        cp = pltpu.make_async_remote_copy(
            src_ref=src,
            dst_ref=ga_ref.at[slot],
            send_sem=as_.at[k],
            recv_sem=ar.at[k],
            device_id=target,
            device_id_type=MESH,
        )
        cp.start()
        acopies[k] = cp

    def token_slot(b, d, e):
        return (b * 2 + d) * 2 + e

    def start_cache(k, src, dst, target):
        cp = pltpu.make_async_remote_copy(
            src_ref=src,
            dst_ref=dst,
            send_sem=cs.at[k],
            recv_sem=cr.at[k],
            device_id=target,
            device_id_type=MESH,
        )
        cp.start()
        return cp

    to_z, to_x, to_c = (zh, 1 - zl, y, c, x), (zh, zl, y, c, 1 - x), (zh, zl, y, 1 - c, x)
    far_pieces = [(f, t) for f in (4, 5, 6, 7) for t in range(3)]
    window = 4
    for f in (0, 1):
        for t in range(3):
            start_weights(f, t)
    for piece in far_pieces[:window]:
        start_weights(*piece)
    for t in range(3):
        start_weights(2, t)
    for t in range(3):
        forward(0, t)

    def modulate_rows(i, carry):
        part = pl.ds(pl.multiple_of(i * 16, 16), 16)
        values = lat_ref[part, :].astype(jnp.float32)
        centred = values - jnp.mean(values, axis=-1, keepdims=True)
        spread = jnp.mean(centred * centred, axis=-1, keepdims=True)
        normed = centred * lax.rsqrt(spread + EPSILON)
        m_ref[part, :] = (normed * gain_ref[...] + shift_ref[...]).astype(jnp.bfloat16)
        return carry

    lax.fori_loop(0, lat_ref.shape[0] // 16, modulate_rows, 0)
    mine = token_slot(zl, c, x)
    start_tokens(0, m_ref, mine, to_z)
    start_tokens(1, m_ref, mine, to_x)
    start_tokens(2, m_ref, mine, to_c)
    local = pltpu.make_async_copy(m_ref, ga_ref.at[mine], ls.at[0])
    local.start()
    for t in range(3):
        start_weights(3, t)
    for t in range(3):
        forward(1, t)
    for p in range(4):
        for t, ref in enumerate((ck_ref, cv_ref)):
            block = ref[:, p * cols : (p + 1) * cols].astype(jnp.float32) * flag_ref[...]
            kept[p, :, t * cols : (t + 1) * cols] = block.astype(jnp.bfloat16)
    cache_c = [start_cache(j, kept.at[2 * j + 1 - c], from_c.at[j], to_c) for j in range(2)]
    for at, piece in enumerate(far_pieces):
        forward(*piece)
        if at + window < len(far_pieces):
            start_weights(*far_pieces[at + window])
        if at == 0:
            for j in range(2):
                cache_c[j].wait()
                halves[j] = kept[2 * j + c] + from_c[j]
            cache_z = start_cache(2, halves.at[1 - zl], from_z, to_z)
        if at in (1, 2, 3):
            forward(2, at - 1)
        if at == 3:
            acopies[0].wait_recv()
            theirs = token_slot(1 - zl, c, x)
            start_tokens(3, ga_ref.at[theirs], theirs, to_x)
            start_tokens(4, ga_ref.at[theirs], theirs, to_c)
        if at in (4, 5, 6):
            forward(3, at - 4)
        if at == 4:
            cache_z.wait()
            part[0] = halves[zl] + from_z[...]
            cache_y = start_cache(3, part.at[0], from_y, (zh, zl, 1 - y, c, x))
        if at == 6:
            acopies[1].wait_recv()
            across = token_slot(zl, c, 1 - x)
            start_tokens(5, ga_ref.at[across], across, to_c)
        if at == 8:
            cache_y.wait()
            part[1] = part[0] + from_y[...]
            cache_zh = start_cache(4, part.at[1], from_zh, (1 - zh, zl, y, c, x))
    acopies[3].wait_recv()
    far = token_slot(1 - zl, c, 1 - x)
    start_tokens(6, ga_ref.at[far], far, to_c)
    cache_zh.wait()
    cache_ref[...] = part[1] + from_zh[...]
    local.wait()
    for k in (2, 4, 5, 6):
        acopies[k].wait_recv()
    for cp in ycopies:
        cp.wait_recv()
    for (f, t), cp in wcopies.items():
        if f:
            cp.wait_send()
    for cp in ycopies:
        cp.wait_send()
    for k in range(7):
        acopies[k].wait_send()


def gather_operands(w_query, w_key, w_value, latents, gain, shift, cache_keys, cache_values, flag):
    rows, half = w_query.shape
    tokens, width = latents.shape
    dma = pltpu.SemaphoreType.DMA
    anywhere = pl.BlockSpec(memory_space=pl.ANY)
    vmem = pl.BlockSpec(memory_space=pltpu.VMEM)
    slab = (cache_keys.shape[0], half // 2)
    bf16 = jnp.bfloat16
    gw, ga, cached = pl.pallas_call(
        gather_kernel,
        out_shape=(
            jax.ShapeDtypeStruct((16, rows, 3 * half // 4), w_query.dtype),
            jax.ShapeDtypeStruct((8, tokens, width), latents.dtype),
            jax.ShapeDtypeStruct(slab, bf16),
        ),
        in_specs=[anywhere] * 3 + [vmem] * 6,
        out_specs=(anywhere, anywhere, vmem),
        scratch_shapes=[
            pltpu.VMEM((tokens, width), bf16),
            pltpu.VMEM((4, *slab), bf16),
            pltpu.VMEM((2, *slab), bf16),
            pltpu.VMEM((2, *slab), bf16),
            pltpu.VMEM(slab, bf16),
            pltpu.VMEM((2, *slab), bf16),
            pltpu.VMEM(slab, bf16),
            pltpu.VMEM(slab, bf16),
            dma((8, 3)),
            dma((8, 3)),
            dma((8, 3)),
            dma((8, 3)),
            dma((7,)),
            dma((7,)),
            dma((1,)),
            dma((5,)),
            dma((5,)),
        ],
        compiler_params=pltpu.CompilerParams(
            collective_id=0, has_side_effects=True, vmem_limit_bytes=32 * 1024 * 1024
        ),
        cost_estimate=pl.CostEstimate(flops=0, bytes_accessed=400_000_000, transcendentals=0),
    )(w_query, w_key, w_value, latents, gain, shift, cache_keys, cache_values, flag)
    return gw.reshape(16 * rows, 3 * half // 4), ga.reshape(8 * tokens, width), cached


def tail_kernel(
    raw_ref, qg_ref, kg_ref, bias_ref, cache_ref, o_ref,
    q_s, k_all, v_all, att, sq, rx, qs, qr, es, er, os_, or_, *, scale, heads, width
):
    zh, zl, y, c, x = (lax.axis_index(a) for a in AXES)
    rows, cols = att.shape[1:]
    head = cols // heads
    tile = rows // 2
    y_here, y_there = (zh, zl, 1 - y, c, x), (1 - zh, zl, 1 - y, c, x)

    def flipped(f):
        return (zh, 1 - zl if f & 4 else zl, y, 1 - c if f & 2 else c, 1 - x if f & 1 else x)

    barrier = pltpu.get_barrier_semaphore()
    partners = [flipped(f) for f in range(1, 8)] + [y_here, y_there]
    for partner in partners:
        pl.semaphore_signal(barrier, inc=1, device_id=partner, device_id_type=MESH)

    for s in range(4):
        part = slice(s * rows, (s + 1) * rows)
        a, b = raw_ref[part, :cols], raw_ref[part, cols : 2 * cols]
        lanes = lax.broadcasted_iota(jnp.int32, (rows, 128), 1)
        both = jnp.where(
            lanes % 8 < 4,
            jnp.sum(a * a, axis=1, keepdims=True),
            jnp.sum(b * b, axis=1, keepdims=True),
        )
        sq[:, part] = both.T[:8]
    for s in range(4):
        v_all[s // 2 * 3 + 1 + s % 2] = raw_ref[s * rows : (s + 1) * rows, 2 * cols :].astype(jnp.bfloat16)
    pl.semaphore_wait(barrier, len(partners))

    copies = []
    for f in range(1, 8):
        cp = pltpu.make_async_remote_copy(
            src_ref=sq,
            dst_ref=rx.at[f],
            send_sem=qs.at[f],
            recv_sem=qr.at[f],
            device_id=flipped(f),
            device_id_type=MESH,
        )
        cp.start()
        copies.append(cp)

    onward = (zh + y - 2 * zh * y, zl, 1 - y, c, x)

    def start_edges(k, ref):
        out = []
        for t, (src, dst, target) in enumerate(((2, y, y_here), (5, 1 - y, onward))):
            cp = pltpu.make_async_remote_copy(
                src_ref=ref.at[src],
                dst_ref=ref.at[dst * 3],
                send_sem=es.at[k, t],
                recv_sem=er.at[k, t],
                device_id=target,
                device_id_type=MESH,
            )
            cp.start()
            out.append(cp)
        return out

    edges = start_edges(0, v_all)
    total = sq[...]
    for f in range(1, 8):
        copies[f - 1].wait_recv()
        total = total + rx[f]
    for s in range(4):
        part = slice(s * rows, (s + 1) * rows)
        sums = jnp.concatenate([total[:, part]] * 16, axis=0).T
        inverse = lax.rsqrt(sums / width + EPSILON)
        k_all[s // 2 * 3 + 1 + s % 2] = (
            raw_ref[part, cols : 2 * cols] * inverse[:, 4:5] * kg_ref[...]
        ).astype(jnp.bfloat16)
        q_s[s] = (raw_ref[part, :cols] * inverse[:, 0:1] * qg_ref[...]).astype(jnp.bfloat16)
    edges += start_edges(1, k_all)

    def attend(n, b, d):
        slot = b * 2 + d

        def one_head(h, carry):
            span = pl.ds(pl.multiple_of(h * head, head), head)
            behind = pl.ds(pl.multiple_of(cols + h * head, head), head)
            old_keys, old_values = cache_ref[:, span], cache_ref[:, behind]
            near_keys = k_all[pl.ds(b * 3 + d, 2), :, span].reshape(2 * rows, head)
            near_values = v_all[pl.ds(b * 3 + d, 2), :, span].reshape(2 * rows, head)
            keys = jnp.concatenate([old_keys, near_keys], axis=0)
            values = jnp.concatenate([old_values, near_values], axis=0)
            query = q_s[slot, :, span]
            for i in range(2):
                scores = lax.dot_general(
                    query[i * tile : (i + 1) * tile],
                    keys,
                    (((1,), (1,)), ((), ())),
                    preferred_element_type=jnp.float32,
                )
                scores = scores * scale + bias_ref[(slot * heads + h) * 2 + i]
                peak = jnp.max(scores, axis=-1, keepdims=True)
                weights = jnp.exp(scores - peak)
                summed = jnp.dot(weights.astype(jnp.bfloat16), values, preferred_element_type=jnp.float32)
                att[n, i * tile : (i + 1) * tile, span] = (
                    summed / jnp.sum(weights, axis=-1, keepdims=True)
                ).astype(jnp.bfloat16)
            return carry

        lax.fori_loop(0, heads, one_head, 0)

    me = zl * 2 + c

    def block(p):
        return o_ref.at[:, pl.ds(pl.multiple_of(p * cols, 128), cols)]

    def push(n, b, d):
        return pltpu.make_async_remote_copy(
            src_ref=att.at[n],
            dst_ref=block(me),
            send_sem=os_.at[n],
            recv_sem=or_.at[me],
            device_id=(zh, b, y, d, x),
            device_id_type=MESH,
        )

    order = [(0, 1 - zl, 1), (1, zl, 1), (2, 1 - zl, 0), (3, zl, 0)]
    for n, b, d in order:
        if n == 2:
            for cp in edges:
                cp.wait_recv()
        attend(n, b, d)
        if n % 2 == 0:
            push(n, b, d).start()
        else:

            @pl.when(c == d)
            def _():
                o_ref[:, pl.ds(pl.multiple_of(me * cols, 128), cols)] = att[n]

            @pl.when(c != d)
            def _():
                push(n, b, d).start()

    for p in ((1 - zl) * 2 + c, zl * 2 + 1 - c, (1 - zl) * 2 + 1 - c):
        pltpu.make_async_remote_copy(
            src_ref=att.at[0],
            dst_ref=block(p),
            send_sem=os_.at[0],
            recv_sem=or_.at[p],
            device_id=flipped(4),
            device_id_type=MESH,
        ).wait_recv()
    for cp in copies + edges:
        cp.wait_send()
    for n, b, d in order:
        if n % 2 == 0:
            push(n, b, d).wait_send()
        else:

            @pl.when(c != d)
            def _():
                push(n, b, d).wait_send()


def attend_groups(raw, q_gain, k_gain, bias, cached, scale, heads, width):
    rows, cols = raw.shape[0] // 4, raw.shape[1] // 3
    dma = pltpu.SemaphoreType.DMA
    bf16 = jnp.bfloat16
    vmem = pl.BlockSpec(memory_space=pltpu.VMEM)
    return pl.pallas_call(
        functools.partial(tail_kernel, scale=scale, heads=heads, width=width),
        out_shape=jax.ShapeDtypeStruct((rows, 4 * cols), bf16),
        in_specs=[vmem] * 5,
        out_specs=vmem,
        scratch_shapes=[
            pltpu.VMEM((4, rows, cols), bf16),
            pltpu.VMEM((6, rows, cols), bf16),
            pltpu.VMEM((6, rows, cols), bf16),
            pltpu.VMEM((4, rows, cols), bf16),
            pltpu.VMEM((8, 4 * rows), jnp.float32),
            pltpu.VMEM((8, 8, 4 * rows), jnp.float32),
            dma((8,)),
            dma((8,)),
            dma((2, 2)),
            dma((2, 2)),
            dma((4,)),
            dma((4,)),
        ],
        compiler_params=pltpu.CompilerParams(
            collective_id=1, has_side_effects=True, vmem_limit_bytes=40 * 1024 * 1024
        ),
    )(raw, q_gain, k_gain, bias, cached)


def local_split(
    latents,
    timesteps,
    mod_shift,
    mod_scale,
    w_query,
    w_key,
    w_value,
    query_gain,
    key_gain,
    cache_keys,
    cache_values,
    owners,
    tile_mask,
):
    zh, zl, y, c, x = (lax.axis_index(a) for a in AXES)
    member = ((zh * 2 + zl) * 2 + y) * 2 + c
    freqs = jnp.exp(-math.log(10000.0) * jnp.arange(latents.shape[1], dtype=jnp.float32) / latents.shape[1])
    angles = timesteps[0].astype(jnp.float32) * freqs
    gain = (1.0 + mod_scale + 0.5 * jnp.cos(angles))[None]
    shift = (mod_shift + 0.5 * jnp.sin(angles))[None]
    root = owners[owners.shape[0] - 1]
    half = w_query.shape[1]
    cols = half // 4
    flag = jnp.full((1, cols), member == root, jnp.float32)
    joined, tokens, cached = gather_operands(
        w_query, w_key, w_value, latents, gain, shift, cache_keys, cache_values, flag
    )
    slab = (zl * 2 + c) * cols
    projected = jnp.dot(tokens, joined, preferred_element_type=jnp.float32)
    q_gain = lax.dynamic_slice_in_dim(query_gain, slab, cols, 0)[None]
    k_gain = lax.dynamic_slice_in_dim(key_gain, slab, cols, 0)[None]
    heads = tile_mask.shape[0] // 4
    query_tiles, key_tiles = tile_mask.shape[1:]
    head = cols // heads
    mask = lax.dynamic_slice_in_dim(tile_mask, (zl * 2 + c) * heads, heads, 0)
    slots = jnp.arange(4)
    group_ids = ((zh * 2 + slots // 2) * 2 + y) * 2 + slots % 2
    tile_ids = jnp.arange(key_tiles)
    earlier = (tile_ids >= query_tiles) & (tile_ids < 2 * query_tiles)
    allowed = jnp.where(
        (group_ids == 0)[:, None, None, None] & earlier[None, None, None, :], 0, mask[None]
    )
    bias = jnp.repeat(jnp.where(allowed > 0, 0.0, -jnp.inf), latents.shape[0], axis=-1)
    bias = bias.reshape(4 * heads * query_tiles, 1, -1).astype(jnp.float32)
    return attend_groups(projected, q_gain, k_gain, bias, cached, 1.0 / math.sqrt(head), heads, 2 * half)


def solution(mesh):
    body, group, tok = local, "group", "tok"
    if mesh.shape["group"] == 16 and mesh.shape["tok"] == 2:
        mesh = jax.sharding.Mesh(mesh.devices.reshape(2, 2, 2, 2, 2), AXES)
        body, group, tok = local_split, ("zh", "zl", "y", "c"), "x"
    both = (*group, tok) if body is local_split else (group, tok)
    return jax.shard_map(
        body,
        mesh=mesh,
        in_specs=(
            P(both, None),
            P(group),
            P(),
            P(),
            P(group, tok),
            P(group, tok),
            P(group, tok),
            P(tok),
            P(tok),
            P(group, tok),
            P(group, tok),
            P(),
            P(tok, None, None),
        ),
        out_specs=P(group, tok),
        check_vma=False,
    )
```

```python
import functools
import math

import jax
import jax.numpy as jnp
from jax import lax
from jax.experimental import pallas as pl
from jax.experimental.pallas import tpu as pltpu
from jax.sharding import PartitionSpec as P

EPSILON = 1e-06
MESH = pl.DeviceIdType.MESH


def from_behind(block, axis, distance):
    devices = range(lax.axis_size(axis))
    route = [(i - distance, i) for i in devices if i - distance in devices]
    return lax.ppermute(block, axis, route)


def spread_2(value, axis, source):
    kept = jnp.where(lax.axis_index(axis) == source, value, 0).astype(value.dtype)
    return lax.psum(kept, axis)


def modulate(rows_block, timestep, mod_shift, mod_scale):
    values = rows_block.astype(jnp.float32)
    width = values.shape[-1]
    centred = values - jnp.mean(values, axis=-1, keepdims=True)
    spread = jnp.mean(centred * centred, axis=-1, keepdims=True)
    normed = centred * lax.rsqrt(spread + EPSILON)
    freqs = jnp.exp(-math.log(10000.0) * jnp.arange(width, dtype=jnp.float32) / width)
    angles = timestep.astype(jnp.float32) * freqs
    return (
        normed * (1.0 + mod_scale + 0.5 * jnp.cos(angles)) + mod_shift + 0.5 * jnp.sin(angles)
    ).astype(jnp.bfloat16)


def scaled_rows(raw, squares, width, gain):
    return (raw * lax.rsqrt(squares / width + EPSILON)[:, None] * gain).astype(jnp.bfloat16)


def dense_attention(query_heads, key_heads, value_heads, allowed, tile_rows, score_scale):
    group_rows = query_heads.shape[1]
    block_rows = 512 if group_rows % 512 == 0 else group_rows
    block_count = group_rows // block_rows
    tiles_per_block = block_rows // tile_rows

    def one_head(operands):
        query_head, key_head, value_head, head_mask = operands
        key_mask = jnp.repeat(head_mask, tile_rows, axis=1)

        def one_block(block_index):
            block_queries = lax.dynamic_slice_in_dim(
                query_head, block_index * block_rows, block_rows, 0
            )
            block_mask = lax.dynamic_slice_in_dim(
                key_mask, block_index * tiles_per_block, tiles_per_block, 0
            )
            row_mask = jnp.repeat(block_mask, tile_rows, axis=0)
            scores = (
                jnp.einsum("id,jd->ij", block_queries, key_head, preferred_element_type=jnp.float32)
                * score_scale
            )
            scores = jnp.where(row_mask > 0, scores, -jnp.inf)
            peak = jnp.max(scores, axis=-1, keepdims=True)
            weights = jnp.exp(scores - peak)
            summed = jnp.dot(
                weights.astype(jnp.bfloat16), value_head, preferred_element_type=jnp.float32
            )
            return (summed / jnp.sum(weights, axis=-1, keepdims=True)).astype(jnp.bfloat16)

        blocks_out = lax.map(one_block, jnp.arange(block_count, dtype=jnp.int32))
        return blocks_out.reshape(group_rows, query_head.shape[1])

    return lax.map(one_head, (query_heads, key_heads, value_heads, allowed))


def local(
    latents,
    timesteps,
    mod_shift,
    mod_scale,
    w_query,
    w_key,
    w_value,
    query_gain,
    key_gain,
    cache_keys,
    cache_values,
    owners,
    tile_mask,
):
    modulated = modulate(latents, timesteps[0], mod_shift, mod_scale)
    root = owners[owners.shape[0] - 1]
    head_cols = w_query.shape[1]
    slabs = (
        lax.all_gather(w_query, "group", axis=0, tiled=True),
        lax.all_gather(w_key, "group", axis=0, tiled=True),
        lax.all_gather(w_value, "group", axis=0, tiled=True),
    )
    joined = jnp.concatenate(slabs, axis=1)
    projected = jnp.dot(
        lax.all_gather(modulated, "tok", axis=0, tiled=True),
        joined,
        preferred_element_type=jnp.float32,
    )
    raw_query = projected[:, :head_cols]
    raw_key = projected[:, head_cols : 2 * head_cols]
    raw_value = projected[:, 2 * head_cols :]
    query_squares, key_squares = lax.psum(
        (jnp.sum(raw_query * raw_query, axis=1), jnp.sum(raw_key * raw_key, axis=1)), "tok"
    )
    width = head_cols * lax.axis_size("tok")
    query_rows = scaled_rows(raw_query, query_squares, width, query_gain)
    key_rows = scaled_rows(raw_key, key_squares, width, key_gain)
    value_rows = raw_value.astype(jnp.bfloat16)
    earlier_keys, earlier_values = from_behind((key_rows, value_rows), "group", 1)
    cached = (spread_2(cache_keys, "group", root), spread_2(cache_values, "group", root))
    group_rows = query_rows.shape[0]
    local_heads = tile_mask.shape[0]
    query_tiles = tile_mask.shape[1]
    key_tile_count = tile_mask.shape[2]
    tile_rows = group_rows // query_tiles
    head_size = head_cols // local_heads
    score_scale = 1.0 / math.sqrt(head_size)
    context_keys = jnp.concatenate([cached[0], earlier_keys, key_rows], axis=0)
    context_values = jnp.concatenate([cached[1], earlier_values, value_rows], axis=0)
    is_first = lax.axis_index("group") == 0
    tile_ids = jnp.arange(key_tile_count, dtype=jnp.int32)
    earlier_region = (tile_ids >= query_tiles) & (tile_ids < 2 * query_tiles)
    allowed = jnp.where(earlier_region[None, None, :] & is_first, 0, tile_mask)
    query_heads = query_rows.reshape(group_rows, local_heads, head_size).transpose(1, 0, 2)
    key_heads = context_keys.reshape(3 * group_rows, local_heads, head_size).transpose(1, 0, 2)
    value_heads = context_values.reshape(3 * group_rows, local_heads, head_size).transpose(1, 0, 2)
    attended = dense_attention(query_heads, key_heads, value_heads, allowed, tile_rows, score_scale)
    return attended.transpose(1, 0, 2).reshape(group_rows, head_cols)


AXES = ("zh", "zl", "y", "c", "x")


def gather_kernel(
    wq_ref, wk_ref, wv_ref, lat_hbm, ck_hbm, cv_hbm, gain_ref, shift_ref, flag_ref, gw_ref, ga_ref, cache_ref,
    m_ref, lat_ref, ck_ref, cv_ref, ins,    kept, from_c, halves, from_z, part, from_y, from_zh, ws, wr, ys, yr, as_, ar, ls, cs, cr
):
    zh, zl, y, c, x = (lax.axis_index(a) for a in AXES)
    weights = (wq_ref, wk_ref, wv_ref)
    rows = wq_ref.shape[0]
    cols = gw_ref.shape[2] // 3

    def flipped(f):
        return (
            1 - zh if f & 4 else zh,
            1 - zl if f & 2 else zl,
            1 - c if f & 1 else c,
        )

    def place(fzh, fzl, fy, fc):
        return ((fzh * 2 + fzl) * 2 + fy) * 2 + fc

    loads = []
    for k, (src, dst) in enumerate(((lat_hbm, lat_ref), (ck_hbm, ck_ref), (cv_hbm, cv_ref))):
        load = pltpu.make_async_copy(src, dst, ins.at[k])
        load.start()
        loads.append(load)
    barrier = pltpu.get_barrier_semaphore()
    partners = [(a, b, y, d, x) for a, b, d in map(flipped, range(1, 8))]
    partners += [(zh, zl, 1 - y, c, x), (zh, zl, y, c, 1 - x)]
    for partner in partners:
        pl.semaphore_signal(barrier, inc=1, device_id=partner, device_id_type=MESH)
    pl.semaphore_wait(barrier, len(partners))

    me = place(zh, zl, y, c)
    wcopies = {}

    def start_weights(f, t):
        a, b, d = flipped(f)
        slab = (b * 2 + d) * cols
        src = weights[t].at[:, pl.ds(pl.multiple_of(slab, 128), cols)]
        dst = gw_ref.at[me, :, pl.ds(t * cols, cols)]
        if f == 0:
            cp = pltpu.make_async_copy(src, dst, wr.at[f, t])
        else:
            cp = pltpu.make_async_remote_copy(
                src_ref=src,
                dst_ref=dst,
                send_sem=ws.at[f, t],
                recv_sem=wr.at[f, t],
                device_id=(a, b, y, d, x),
                device_id_type=MESH,
            )
        cp.start()
        wcopies[f, t] = cp

    ycopies = []

    def forward(f, t):
        if f == 0:
            wcopies[f, t].wait()
        else:
            wcopies[f, t].wait_recv()
        a, b, d = flipped(f)
        piece = gw_ref.at[place(a, b, y, d), :, pl.ds(t * cols, cols)]
        cp = pltpu.make_async_remote_copy(
            src_ref=piece,
            dst_ref=piece,
            send_sem=ys.at[f, t],
            recv_sem=yr.at[f, t],
            device_id=(zh, zl, 1 - y, c, x),
            device_id_type=MESH,
        )
        cp.start()
        ycopies.append(cp)

    acopies = {}

    def start_tokens(k, src, slot, target):
        cp = pltpu.make_async_remote_copy(
            src_ref=src,
            dst_ref=ga_ref.at[slot],
            send_sem=as_.at[k],
            recv_sem=ar.at[k],
            device_id=target,
            device_id_type=MESH,
        )
        cp.start()
        acopies[k] = cp

    def token_slot(b, d, e):
        return (b * 2 + d) * 2 + e

    def start_cache(k, src, dst, target):
        cp = pltpu.make_async_remote_copy(
            src_ref=src,
            dst_ref=dst,
            send_sem=cs.at[k],
            recv_sem=cr.at[k],
            device_id=target,
            device_id_type=MESH,
        )
        cp.start()
        return cp

    to_z, to_x, to_c = (zh, 1 - zl, y, c, x), (zh, zl, y, c, 1 - x), (zh, zl, y, 1 - c, x)
    few = from_y.shape[0]
    held = pl.ds(pl.multiple_of(y * few, few), few)
    sent = pl.ds(pl.multiple_of((1 - y) * few, few), few)
    far_pieces = [(f, t) for f in (4, 5, 6, 7) for t in range(3)]
    window = 4
    for f in (0, 1):
        for t in range(3):
            start_weights(f, t)
    for piece in far_pieces[:window]:
        start_weights(*piece)
    for t in range(3):
        start_weights(2, t)
    for t in range(3):
        forward(0, t)

    def modulate_rows(i, carry):
        part = pl.ds(pl.multiple_of(i * 16, 16), 16)
        values = lat_ref[part, :].astype(jnp.float32)
        centred = values - jnp.mean(values, axis=-1, keepdims=True)
        spread = jnp.mean(centred * centred, axis=-1, keepdims=True)
        normed = centred * lax.rsqrt(spread + EPSILON)
        m_ref[part, :] = (normed * gain_ref[...] + shift_ref[...]).astype(jnp.bfloat16)
        return carry

    loads[0].wait()
    lax.fori_loop(0, lat_ref.shape[0] // 16, modulate_rows, 0)
    mine = token_slot(zl, c, x)
    start_tokens(0, m_ref, mine, to_z)
    start_tokens(1, m_ref, mine, to_x)
    start_tokens(2, m_ref, mine, to_c)
    local = pltpu.make_async_copy(m_ref, ga_ref.at[mine], ls.at[0])
    local.start()
    for t in range(3):
        start_weights(3, t)
    for t in range(3):
        forward(1, t)
    loads[1].wait()
    loads[2].wait()
    for p in range(4):
        for t, ref in enumerate((ck_ref, cv_ref)):
            block = ref[:, p * cols : (p + 1) * cols].astype(jnp.float32) * flag_ref[...]
            kept[p, :, t * cols : (t + 1) * cols] = block.astype(jnp.bfloat16)
    cache_c = [start_cache(j, kept.at[2 * j + 1 - c], from_c.at[j], to_c) for j in range(2)]
    for at, piece in enumerate(far_pieces):
        forward(*piece)
        if at + window < len(far_pieces):
            start_weights(*far_pieces[at + window])
        if at == 0:
            for j in range(2):
                cache_c[j].wait()
                halves[j] = kept[2 * j + c] + from_c[j]
            cache_z = start_cache(2, halves.at[1 - zl], from_z, to_z)
        if at in (1, 2, 3):
            forward(2, at - 1)
        if at == 3:
            acopies[0].wait_recv()
            theirs = token_slot(1 - zl, c, x)
            start_tokens(3, ga_ref.at[theirs], theirs, to_x)
            start_tokens(4, ga_ref.at[theirs], theirs, to_c)
        if at in (4, 5, 6):
            forward(3, at - 4)
        if at == 4:
            cache_z.wait()
            part[0] = halves[zl] + from_z[...]
            cache_y = start_cache(3, part.at[0, sent], from_y, (zh, zl, 1 - y, c, x))
        if at == 6:
            acopies[1].wait_recv()
            across = token_slot(zl, c, 1 - x)
            start_tokens(5, ga_ref.at[across], across, to_c)
        if at == 6:
            cache_y.wait()
            part[1, held] = part[0, held] + from_y[...]
            cache_zh = start_cache(4, part.at[1, held], from_zh, (1 - zh, zl, y, c, x))
        if at == 9:
            cache_zh.wait()
            cache_ref[held] = part[1, held] + from_zh[...]
            half = cache_ref.at[held]
            cache_last = start_cache(5, half, half, (zh, zl, 1 - y, c, x))
    acopies[3].wait_recv()
    far = token_slot(1 - zl, c, 1 - x)
    start_tokens(6, ga_ref.at[far], far, to_c)
    cache_last.wait()
    local.wait()
    for k in (2, 4, 5, 6):
        acopies[k].wait_recv()
    for cp in ycopies:
        cp.wait_recv()
    for (f, t), cp in wcopies.items():
        if f:
            cp.wait_send()
    for cp in ycopies:
        cp.wait_send()
    for k in range(7):
        acopies[k].wait_send()


def gather_operands(w_query, w_key, w_value, latents, cache_keys, cache_values, gain, shift, flag):
    rows, half = w_query.shape
    tokens, width = latents.shape
    dma = pltpu.SemaphoreType.DMA
    anywhere = pl.BlockSpec(memory_space=pl.ANY)
    vmem = pl.BlockSpec(memory_space=pltpu.VMEM)
    slab = (cache_keys.shape[0], half // 2)
    bf16 = jnp.bfloat16
    gw, ga, cached = pl.pallas_call(
        gather_kernel,
        out_shape=(
            jax.ShapeDtypeStruct((16, rows, 3 * half // 4), w_query.dtype),
            jax.ShapeDtypeStruct((8, tokens, width), latents.dtype),
            jax.ShapeDtypeStruct(slab, bf16),
        ),
        in_specs=[anywhere] * 6 + [vmem] * 3,
        out_specs=(anywhere, anywhere, vmem),
        scratch_shapes=[
            pltpu.VMEM((tokens, width), bf16),
            pltpu.VMEM((tokens, width), bf16),
            pltpu.VMEM(cache_keys.shape, bf16),
            pltpu.VMEM(cache_keys.shape, bf16),
            dma((3,)),
            pltpu.VMEM((4, *slab), bf16),
            pltpu.VMEM((2, *slab), bf16),
            pltpu.VMEM((2, *slab), bf16),
            pltpu.VMEM(slab, bf16),
            pltpu.VMEM((2, *slab), bf16),
            pltpu.VMEM((slab[0] // 2, slab[1]), bf16),
            pltpu.VMEM((slab[0] // 2, slab[1]), bf16),
            dma((8, 3)),
            dma((8, 3)),
            dma((8, 3)),
            dma((8, 3)),
            dma((7,)),
            dma((7,)),
            dma((1,)),
            dma((6,)),
            dma((6,)),
        ],
        compiler_params=pltpu.CompilerParams(
            collective_id=0, has_side_effects=True, vmem_limit_bytes=56 * 1024 * 1024
        ),
        cost_estimate=pl.CostEstimate(flops=0, bytes_accessed=400_000_000, transcendentals=0),
    )(w_query, w_key, w_value, latents, cache_keys, cache_values, gain, shift, flag)
    return gw.reshape(16 * rows, 3 * half // 4), ga.reshape(8 * tokens, width), cached


def tail_kernel(
    raw_ref, qg_ref, kg_ref, bias_ref, cache_ref, o_ref,
    q_s, k_all, v_all, att, sq, rx, qs, qr, es, er, os_, or_, *, scale, heads, width
):
    zh, zl, y, c, x = (lax.axis_index(a) for a in AXES)
    rows, cols = att.shape[1:]
    head = cols // heads
    tile = rows // 2
    y_here, y_there = (zh, zl, 1 - y, c, x), (1 - zh, zl, 1 - y, c, x)

    def flipped(f):
        return (zh, 1 - zl if f & 4 else zl, y, 1 - c if f & 2 else c, 1 - x if f & 1 else x)

    barrier = pltpu.get_barrier_semaphore()
    partners = [flipped(f) for f in range(1, 8)] + [y_here, y_there]
    for partner in partners:
        pl.semaphore_signal(barrier, inc=1, device_id=partner, device_id_type=MESH)

    for s in range(4):
        part = slice(s * rows, (s + 1) * rows)
        a, b = raw_ref[part, :cols], raw_ref[part, cols : 2 * cols]
        lanes = lax.broadcasted_iota(jnp.int32, (rows, 128), 1)
        both = jnp.where(
            lanes % 8 < 4,
            jnp.sum(a * a, axis=1, keepdims=True),
            jnp.sum(b * b, axis=1, keepdims=True),
        )
        sq[:, part] = both.T[:8]
    for s in range(4):
        v_all[s // 2 * 3 + 1 + s % 2] = raw_ref[s * rows : (s + 1) * rows, 2 * cols :].astype(jnp.bfloat16)
    pl.semaphore_wait(barrier, len(partners))

    copies = []
    for f in range(1, 8):
        cp = pltpu.make_async_remote_copy(
            src_ref=sq,
            dst_ref=rx.at[f],
            send_sem=qs.at[f],
            recv_sem=qr.at[f],
            device_id=flipped(f),
            device_id_type=MESH,
        )
        cp.start()
        copies.append(cp)

    onward = (zh + y - 2 * zh * y, zl, 1 - y, c, x)

    def start_edges(k, ref):
        out = []
        for t, (src, dst, target) in enumerate(((2, y, y_here), (5, 1 - y, onward))):
            cp = pltpu.make_async_remote_copy(
                src_ref=ref.at[src],
                dst_ref=ref.at[dst * 3],
                send_sem=es.at[k, t],
                recv_sem=er.at[k, t],
                device_id=target,
                device_id_type=MESH,
            )
            cp.start()
            out.append(cp)
        return out

    edges = start_edges(0, v_all)
    total = sq[...]
    for f in range(1, 8):
        copies[f - 1].wait_recv()
        total = total + rx[f]
    for s in range(4):
        part = slice(s * rows, (s + 1) * rows)
        sums = jnp.concatenate([total[:, part]] * 16, axis=0).T
        inverse = lax.rsqrt(sums / width + EPSILON)
        k_all[s // 2 * 3 + 1 + s % 2] = (
            raw_ref[part, cols : 2 * cols] * inverse[:, 4:5] * kg_ref[...]
        ).astype(jnp.bfloat16)
        q_s[s] = (raw_ref[part, :cols] * inverse[:, 0:1] * qg_ref[...]).astype(jnp.bfloat16)
    edges += start_edges(1, k_all)

    def attend(n, b, d):
        slot = b * 2 + d

        def one_head(h, carry):
            span = pl.ds(pl.multiple_of(h * head, head), head)
            behind = pl.ds(pl.multiple_of(cols + h * head, head), head)
            old_keys, old_values = cache_ref[:, span], cache_ref[:, behind]
            near_keys = k_all[pl.ds(b * 3 + d, 2), :, span].reshape(2 * rows, head)
            near_values = v_all[pl.ds(b * 3 + d, 2), :, span].reshape(2 * rows, head)
            keys = jnp.concatenate([old_keys, near_keys], axis=0)
            values = jnp.concatenate([old_values, near_values], axis=0)
            query = q_s[slot, :, span]
            for i in range(2):
                scores = lax.dot_general(
                    query[i * tile : (i + 1) * tile],
                    keys,
                    (((1,), (1,)), ((), ())),
                    preferred_element_type=jnp.float32,
                )
                scores = scores * scale + bias_ref[(slot * heads + h) * 2 + i]
                peak = jnp.max(scores, axis=-1, keepdims=True)
                weights = jnp.exp(scores - peak)
                summed = jnp.dot(weights.astype(jnp.bfloat16), values, preferred_element_type=jnp.float32)
                att[n, i * tile : (i + 1) * tile, span] = (
                    summed / jnp.sum(weights, axis=-1, keepdims=True)
                ).astype(jnp.bfloat16)
            return carry

        lax.fori_loop(0, heads, one_head, 0)

    me = zl * 2 + c

    def block(p):
        return o_ref.at[:, pl.ds(pl.multiple_of(p * cols, 128), cols)]

    def push(n, b, d):
        return pltpu.make_async_remote_copy(
            src_ref=att.at[n],
            dst_ref=block(me),
            send_sem=os_.at[n],
            recv_sem=or_.at[me],
            device_id=(zh, b, y, d, x),
            device_id_type=MESH,
        )

    order = [(0, 1 - zl, 1), (1, zl, 1), (2, 1 - zl, 0), (3, zl, 0)]
    for n, b, d in order:
        if n == 2:
            for cp in edges:
                cp.wait_recv()
        attend(n, b, d)
        if n % 2 == 0:
            push(n, b, d).start()
        else:

            @pl.when(c == d)
            def _():
                o_ref[:, pl.ds(pl.multiple_of(me * cols, 128), cols)] = att[n]

            @pl.when(c != d)
            def _():
                push(n, b, d).start()

    for p in ((1 - zl) * 2 + c, zl * 2 + 1 - c, (1 - zl) * 2 + 1 - c):
        pltpu.make_async_remote_copy(
            src_ref=att.at[0],
            dst_ref=block(p),
            send_sem=os_.at[0],
            recv_sem=or_.at[p],
            device_id=flipped(4),
            device_id_type=MESH,
        ).wait_recv()
    for cp in copies + edges:
        cp.wait_send()
    for n, b, d in order:
        if n % 2 == 0:
            push(n, b, d).wait_send()
        else:

            @pl.when(c != d)
            def _():
                push(n, b, d).wait_send()


def attend_groups(raw, q_gain, k_gain, bias, cached, scale, heads, width):
    rows, cols = raw.shape[0] // 4, raw.shape[1] // 3
    dma = pltpu.SemaphoreType.DMA
    bf16 = jnp.bfloat16
    vmem = pl.BlockSpec(memory_space=pltpu.VMEM)
    return pl.pallas_call(
        functools.partial(tail_kernel, scale=scale, heads=heads, width=width),
        out_shape=jax.ShapeDtypeStruct((rows, 4 * cols), bf16),
        in_specs=[vmem] * 5,
        out_specs=vmem,
        scratch_shapes=[
            pltpu.VMEM((4, rows, cols), bf16),
            pltpu.VMEM((6, rows, cols), bf16),
            pltpu.VMEM((6, rows, cols), bf16),
            pltpu.VMEM((4, rows, cols), bf16),
            pltpu.VMEM((8, 4 * rows), jnp.float32),
            pltpu.VMEM((8, 8, 4 * rows), jnp.float32),
            dma((8,)),
            dma((8,)),
            dma((2, 2)),
            dma((2, 2)),
            dma((4,)),
            dma((4,)),
        ],
        compiler_params=pltpu.CompilerParams(
            collective_id=1, has_side_effects=True, vmem_limit_bytes=20 * 1024 * 1024
        ),
    )(raw, q_gain, k_gain, bias, cached)


def local_split(
    latents,
    timesteps,
    mod_shift,
    mod_scale,
    w_query,
    w_key,
    w_value,
    query_gain,
    key_gain,
    cache_keys,
    cache_values,
    owners,
    tile_mask,
):
    zh, zl, y, c, x = (lax.axis_index(a) for a in AXES)
    member = ((zh * 2 + zl) * 2 + y) * 2 + c
    freqs = jnp.exp(-math.log(10000.0) * jnp.arange(latents.shape[1], dtype=jnp.float32) / latents.shape[1])
    angles = timesteps[0].astype(jnp.float32) * freqs
    gain = (1.0 + mod_scale + 0.5 * jnp.cos(angles))[None]
    shift = (mod_shift + 0.5 * jnp.sin(angles))[None]
    root = owners[owners.shape[0] - 1]
    half = w_query.shape[1]
    cols = half // 4
    flag = jnp.full((1, cols), member == root, jnp.float32)
    joined, tokens, cached = gather_operands(
        w_query, w_key, w_value, latents, cache_keys, cache_values, gain, shift, flag
    )
    slab = (zl * 2 + c) * cols
    projected = jnp.dot(tokens, joined, preferred_element_type=jnp.float32)
    q_gain = lax.dynamic_slice_in_dim(query_gain, slab, cols, 0)[None]
    k_gain = lax.dynamic_slice_in_dim(key_gain, slab, cols, 0)[None]
    heads = tile_mask.shape[0] // 4
    query_tiles, key_tiles = tile_mask.shape[1:]
    head = cols // heads
    mask = lax.dynamic_slice_in_dim(tile_mask, (zl * 2 + c) * heads, heads, 0)
    slots = jnp.arange(4)
    group_ids = ((zh * 2 + slots // 2) * 2 + y) * 2 + slots % 2
    tile_ids = jnp.arange(key_tiles)
    earlier = (tile_ids >= query_tiles) & (tile_ids < 2 * query_tiles)
    allowed = jnp.where(
        (group_ids == 0)[:, None, None, None] & earlier[None, None, None, :], 0, mask[None]
    )
    bias = jnp.repeat(jnp.where(allowed > 0, 0.0, -jnp.inf), latents.shape[0], axis=-1)
    bias = bias.reshape(4 * heads * query_tiles, 1, -1).astype(jnp.float32)
    return attend_groups(projected, q_gain, k_gain, bias, cached, 1.0 / math.sqrt(head), heads, 2 * half)


def solution(mesh):
    body, group, tok = local, "group", "tok"
    if mesh.shape["group"] == 16 and mesh.shape["tok"] == 2:
        mesh = jax.sharding.Mesh(mesh.devices.reshape(2, 2, 2, 2, 2), AXES)
        body, group, tok = local_split, ("zh", "zl", "y", "c"), "x"
    both = (*group, tok) if body is local_split else (group, tok)
    return jax.shard_map(
        body,
        mesh=mesh,
        in_specs=(
            P(both, None),
            P(group),
            P(),
            P(),
            P(group, tok),
            P(group, tok),
            P(group, tok),
            P(tok),
            P(tok),
            P(group, tok),
            P(group, tok),
            P(),
            P(tok, None, None),
        ),
        out_specs=P(group, tok),
        check_vma=False,
    )
```
